256 devices in a mesh: ctx: 16 (over x, z_lo, core), exp: 16 (over y, z_hi).
Axes of the slice: x: 4, y: 4, z: 8 (z_hi: 4, z_lo: 2; z = z_hi * 2 + z_lo), core: 2. Of those that a mesh axis runs over, the one named last changes fastest.
Arguments:
- queries: bfloat16 [2048, 64, 192], P('ctx', 'exp'), may hold values from -8 to 8
- latent_cache: bfloat16 [4096, 576], P('ctx'), may hold values from -8 to 8
- group_latent: bfloat16 [2048, 576], P('ctx'), may hold values from -6 to 6
- w_absorb_k: bfloat16 [64, 128, 512], P('exp'), may hold values from -0.5 to 0.5
- value_absorb_weight: bfloat16 [64, 512, 128], P('exp'), may hold values from -1 to 1
- w_out: bfloat16 [8192, 7168], P('exp', 'ctx'), may hold values from -0.1875 to 0.1875
- residual: bfloat16 [2048, 7168], P('exp', 'ctx'), may hold values from -12 to 12
- norm_gain: float32 [7168], P('ctx'), may hold values from 0.5 to 1.5
- routes: int32 [2048, 1], P('exp'), may hold values from 0 to 15; in each aligned block of 128 rows (0 to 127, 128 to 255, ...) at most 16 rows name the same one
- route_weight: float32 [2048, 1], P('exp'), may hold values from 0.3 to 3
- w_gate: bfloat16 [16, 7168, 2048], P('exp', 'ctx'), may hold values from -0.0625 to 0.0625
- w_up: bfloat16 [16, 7168, 2048], P('exp', 'ctx'), may hold values from -0.0625 to 0.0625
- w_down: bfloat16 [16, 2048, 7168], P('exp', None, 'ctx'), may hold values from -0.125 to 0.125
Outputs:
- mixed: bfloat16 [2048, 7168], P('exp', 'ctx')
The draws below stay inside these ranges and needn't reach their ends.
Inputs may be any that keep to these rules, and one draw needn't show every extreme that they name: `routes`: in each aligned block of 128 rows (the rows of one exp index), no expert is named by more than 16 rows, a bound that some block reaches.
All inputs are finite; a program needn't handle non-finite values.
Results may differ from the reference program's by a relative error of at most 0.022.
Values may be sent and summed in bfloat16 or wider, within the bound.
A program may use at most 64 MiB of HBM per device.

```python
import math
import jax
import jax.numpy as jnp
import numpy as np
from jax import lax

D = 7168
HEADS = 64
NOPE = 128
ROPE = 64
KV_RANK = 512
V_DIM = 128
FF = 2048
TOP = 1
CAP = 16
EXPERTS = 16
GROUP = 2048
CACHE = 4096
TOK_EXP = 128
N_EXP = 16


def draw_queries(key, part):
    key = jax.random.fold_in(key, 11)
    values = jnp.clip(jax.random.normal(key, (GROUP, HEADS, NOPE + ROPE), jnp.float32), -6.0, 6.0)
    return values.astype(jnp.bfloat16)


def draw_latent_cache(key, part):
    key = jax.random.fold_in(key, 23)
    values = jnp.clip(jax.random.normal(key, (CACHE, KV_RANK + ROPE), jnp.float32), -6.0, 6.0)
    return values.astype(jnp.bfloat16)


def column_scale(rise):
    fraction = jnp.arange(D).astype(jnp.float32) / (D - 1)
    return 0.5 * jnp.exp(math.log(rise) * fraction)


def draw_residual(key, part):
    key = jax.random.fold_in(key, 37)
    values = jnp.clip(jax.random.normal(key, (GROUP, D), jnp.float32), -4.5, 4.5) * column_scale(5.0)[None, :]
    return values.astype(jnp.bfloat16)


def steps_of(rng, dims, pieces, least, top_value):
    level = 1.0
    for dim, parts in pieces:
        heights = jax.random.uniform(jax.random.fold_in(jax.random.fold_in(rng, 6), dim), (parts,), jnp.float32, least / len(pieces), top_value / len(pieces))
        level = level * jnp.repeat(jnp.exp(heights), dims[dim] // parts).reshape((-1,) + (1,) * (len(dims) - 1 - dim))
    return level


def routed_block(key, own, number, rows, number_of, top, limit, slope):
    order = jax.random.permutation(key, number_of)
    crowded, ordinary = shares(number_of, rows * top, limit, slope, True), shares(number_of, rows * top, limit, slope, False)
    places = jnp.arange(number_of)

    def named(sizes, rotation):
        used = int((sizes > 0).sum())
        fixed = max(1, used // 4)
        shifted = fixed + (places - fixed + rotation * (used - fixed)) % max(1, number_of - fixed)
        return jnp.zeros((number_of,), jnp.int32).at[order[jnp.where(places < fixed, places, shifted)]].set(jnp.asarray(sizes, jnp.int32))

    sizes = jnp.where(number % 4 == 0, named(crowded, number // 4), named(ordinary, number - number // 4 - 1))
    mixed = jax.random.permutation(jax.random.fold_in(own, 3), number_of)
    source_of, sink = mixed[0:number_of // 2 * 2:2], mixed[1:number_of // 2 * 2:2]
    margin = jnp.minimum(sizes[source_of] - 1, limit - sizes[sink]) // 2
    margin = jnp.where((source_of == order[0]) | (sink == order[0]) | (sizes[sink] == 0), 0, jnp.maximum(margin, 0))
    shifted = jax.random.randint(jax.random.fold_in(own, 4), (number_of // 2,), 0, 1 << 20) % (margin + 1)
    sizes = sizes.at[source_of].add(-shifted).at[sink].add(shifted)
    labels = jnp.searchsorted(jnp.cumsum(sizes), jnp.arange(rows * top), side="right").astype(jnp.int32)
    grid = labels.reshape(top, rows).T
    grid = grid[jax.random.permutation(jax.random.fold_in(own, 1), rows)]
    rotation = jax.random.randint(jax.random.fold_in(own, 2), (rows, 1), 0, top)
    return jnp.take_along_axis(grid, (jnp.arange(top)[None, :] + rotation) % top, axis=1)


def shares(amount, total, bound, skew, full):
    loads = [(1 << 20) // math.isqrt(grade ** skew) + 1 for grade in range(1, amount + 1)]
    largest = bound if full else min(bound, max(-(-total // amount), total * loads[0] // sum(loads)))
    least = 1 if total - largest >= amount - 1 else 0
    given, surplus = [largest] + [least] * (amount - 1), total - largest - least * (amount - 1)
    while surplus > 0:
        free = [i for i in range(1, amount) if given[i] < largest] or [i for i in range(1, amount) if given[i] < bound]
        mass, budget = sum([loads[i] for i in free]), surplus
        for i in free:
            extra = min(bound - given[i], max(1, budget * loads[i] // mass), surplus)
            given[i] = given[i] + extra
            surplus = surplus - extra
    return np.array(given)


def centred(key, dims, scale, reach, split=(), held_as=jnp.bfloat16):
    array = scale * jax.random.normal(key, dims, jnp.float32)
    if split:
        array = array * steps_of(key, dims, split, -0.22, 0.18)
    return jnp.clip(array, -reach, reach).astype(held_as)


def setup_inputs(seed: int = 0) -> dict:
    key_of = jax.random.split(jax.random.key(seed), 14)
    queries = draw_queries(jax.random.fold_in(key_of[13], 71), 0)
    latent_cache = draw_latent_cache(jax.random.fold_in(key_of[13], 71), 0)
    group_latent = centred(key_of[2], (GROUP, KV_RANK + ROPE), 1.0, 6.0, ((0, 16),))
    w_absorb_k = centred(key_of[3], (HEADS, NOPE, KV_RANK), NOPE ** -0.5, 0.5, ((0, 16),))
    value_absorb_weight = centred(key_of[4], (HEADS, KV_RANK, V_DIM), (KV_RANK // 16) ** -0.5, 1.0, ((0, 16),))
    w_out = centred(key_of[5], (HEADS * V_DIM, D), (HEADS * V_DIM // 8) ** -0.5, 0.1875, ((0, 16), (1, 16)))
    residual = draw_residual(jax.random.fold_in(key_of[13], 71), 0)
    norm_gain = jnp.clip(1.0 + 0.1 * jax.random.normal(key_of[7], (D,), jnp.float32), 0.5, 1.5)
    routes_keys = jax.random.split(jax.random.fold_in(key_of[8], 1), GROUP // TOK_EXP)
    routes_turns = jax.random.permutation(jax.random.fold_in(key_of[8], 3), GROUP // TOK_EXP)
    routes = jax.vmap(lambda own, number: routed_block(jax.random.fold_in(key_of[8], 2), own, number, TOK_EXP, EXPERTS, TOP, CAP, 2))(routes_keys, routes_turns).reshape((GROUP, TOP))
    route_weight = jnp.clip(jnp.exp(math.log(3.0) - 2.3025851 * jax.random.uniform(key_of[9], (GROUP, TOP), jnp.float32) ** steps_of(key_of[9], (GROUP, TOP), ((0, 16),), -0.2, 0.2)), 0.3, 3.0)
    w_gate = centred(key_of[10], (EXPERTS, D, FF), D ** -0.5, 0.0625, ((0, 16), (1, 16)))
    w_up = centred(key_of[11], (EXPERTS, D, FF), D ** -0.5, 0.0625, ((0, 16), (1, 16)))
    w_down = centred(key_of[12], (EXPERTS, FF, D), FF ** -0.5, 0.125, ((0, 16), (2, 16)))
    return {"queries": queries, "latent_cache": latent_cache, "group_latent": group_latent, "w_absorb_k": w_absorb_k, "value_absorb_weight": value_absorb_weight, "w_out": w_out, "residual": residual, "norm_gain": norm_gain, "routes": routes, "route_weight": route_weight, "w_gate": w_gate, "w_up": w_up, "w_down": w_down}


def slot_matrix(route_row):
    onehot = (route_row[:, None] == jnp.arange(EXPERTS)[None, :]).astype(jnp.int32)
    earlier = jnp.cumsum(onehot, axis=0) - onehot
    slot = lax.optimization_barrier(jnp.sum(earlier * onehot, axis=1))
    target = route_row * CAP + slot
    return (jnp.arange(EXPERTS * CAP)[:, None] == target[None, :]).astype(jnp.float32)

def reference(queries, latent_cache, group_latent, w_absorb_k, value_absorb_weight, w_out, residual, norm_gain, routes, route_weight, w_gate, w_up, w_down):
    lowered = jnp.einsum('thn,hnk->thk', queries[:, :, :NOPE].astype(jnp.float32), w_absorb_k.astype(jnp.float32)).astype(jnp.bfloat16)
    absorbed_query = jnp.concatenate([lowered, queries[:, :, NOPE:]], axis=2)
    keys = jnp.concatenate([latent_cache, group_latent], axis=0)
    inverse_scale = 1.0 / math.sqrt(NOPE + ROPE)
    column = jnp.arange(CACHE + GROUP)[None, :]
    position = jnp.arange(GROUP)[:, None]
    visible = (column < CACHE) | (column - CACHE <= position)

    def head_context(query_rows):
        scores = lax.dot_general(query_rows, keys, (((1,), (1,)), ((), ())), preferred_element_type=jnp.float32) * inverse_scale
        masked = jnp.where(visible, scores, -1e+30)
        peak = lax.optimization_barrier(jnp.max(masked, axis=1))
        weights = jnp.where(visible, jnp.exp(masked - peak[:, None]), 0.0)
        total = lax.optimization_barrier(jnp.sum(weights, axis=1))
        numerator = jnp.dot(weights.astype(jnp.bfloat16), keys[:, :KV_RANK], preferred_element_type=jnp.float32)
        return (numerator / total[:, None]).astype(jnp.bfloat16)
    context_vectors = lax.map(head_context, jnp.transpose(absorbed_query, (1, 0, 2)))
    per_head_output = jnp.einsum('qwi,qic->wqc', context_vectors.astype(jnp.float32), value_absorb_weight.astype(jnp.float32)).astype(jnp.bfloat16)
    per_head_output = per_head_output.reshape(GROUP, HEADS * V_DIM)
    attended = jnp.dot(per_head_output, w_out, preferred_element_type=jnp.float32)
    state = residual.astype(jnp.float32) + attended
    mean_square = lax.optimization_barrier(jnp.sum(state * state, axis=1)) / D
    normed = (state * lax.rsqrt(mean_square + 1e-06)[:, None] * norm_gain[None, :]).astype(jnp.bfloat16)
    matrices = jax.vmap(slot_matrix)(routes.reshape(N_EXP, TOK_EXP * TOP))
    pairs = jnp.repeat(normed, TOP, axis=0).reshape(N_EXP, TOK_EXP * TOP, D)
    dispatch = jnp.einsum('bsp,bpd->bsd', matrices, pairs.astype(jnp.float32)).astype(jnp.bfloat16)
    rows = dispatch.reshape(N_EXP, EXPERTS, CAP, D).transpose(1, 0, 2, 3).reshape(EXPERTS, N_EXP * CAP, D)

    def expert(items):
        expert_rows, gate_weight, up_weight, down_projection_weight = items
        gate = jnp.dot(expert_rows, gate_weight, preferred_element_type=jnp.float32)
        up = jnp.dot(expert_rows, up_weight, preferred_element_type=jnp.float32)
        hidden = (jax.nn.silu(gate) * up).astype(jnp.bfloat16)
        return jnp.dot(hidden, down_projection_weight, preferred_element_type=jnp.float32).astype(jnp.bfloat16)
    results = lax.map(expert, (rows, w_gate, w_up, w_down))
    back = results.reshape(EXPERTS, N_EXP, CAP, D).transpose(1, 0, 2, 3).reshape(N_EXP, EXPERTS * CAP, D)
    token_out = jnp.einsum('bsp,bsd->bpd', matrices, back.astype(jnp.float32)).reshape(GROUP, TOP, D)
    routed = lax.optimization_barrier(jnp.sum(token_out * route_weight[:, :, None], axis=1))
    return (state + routed).astype(jnp.bfloat16)
```

```python
import math

import jax
import jax.numpy as jnp
from jax import lax
from jax.experimental import pallas as pl
from jax.experimental.pallas import tpu as pltpu
from jax.sharding import PartitionSpec as P

MESH = pl.DeviceIdType.MESH
F32 = jnp.float32
BF16 = jnp.bfloat16
D = 7168
CAP = 16
HEADS = 4
TOK = 128
NOPE = 128
RANK = 512
VD = 128
WIDTH = 448
FF = 2048
HALF = FF // 2
CACHE = 256
GROUP = 128
KEYS = CACHE + GROUP
KW = RANK + 128
SCALE = 1.0 / math.sqrt(192.0) * math.log2(math.e)


def mm(a, b):
    return jnp.dot(a, b, preferred_element_type=F32)


def kernel(
    q_ref,
    cache_ref,
    group_ref,
    wk_ref,
    wv_ref,
    wo_ref,
    res_ref,
    gain_ref,
    rt_ref,
    rw_ref,
    wg_ref,
    wu_ref,
    wd_ref,
    out_ref,
    qbuf,
    kbuf,
    qabuf,
    acc,
    mbuf,
    lbuf,
    osend,
    ssend,
    orecv,
    srecv,
    agbuf,
    wbuf,
    rsend,
    rrecv,
    state,
    dsend,
    drecv,
    gubuf,
    wdbuf,
    psend,
    precv,
    hid,
    ysend,
    yrecv,
    sem_q,
    sem_k,
    sem_w,
    sem_gu,
    sem_wd,
    sem_o,
    sem_s,
    sem_ag,
    sem_f,
    sem_rs,
    sem_d,
    sem_df,
    sem_p,
    sem_h,
    sem_hf,
    sem_y,
):
    c = lax.axis_index("ctx")
    e = lax.axis_index("exp")
    x, zl, k = c // 4, (c // 2) % 2, c % 2
    y, zh = e // 4, e % 4
    z = 2 * zh + zl

    def at(x_, zl_, k_, y_, zh_):
        return (x_ * 4 + zl_ * 2 + k_, y_ * 4 + zh_)

    def at_z(z_):
        return at(x, z_ % 2, k, y, z_ // 2)

    sibling = at(x, zl, 1 - k, y, zh)
    z_up = at_z((z + 1) % 8)
    z_down = at_z((z + 7) % 8)
    diagonal = x == y

    def remote(src, dst, sems, i, device):
        return pltpu.make_async_remote_copy(
            src_ref=src,
            dst_ref=dst,
            send_sem=sems.at[0, i],
            recv_sem=sems.at[1, i],
            device_id=device,
            device_id_type=MESH,
        )

    barrier = pltpu.get_barrier_semaphore()

    def hello(device):
        pl.semaphore_signal(barrier, inc=1, device_id=device, device_id_type=MESH)

    for d in (1, 3, 2):
        hello(at((x + d) % 4, zl, k, y, zh))
        hello(at(x, zl, k, (y + d) % 4, zh))
    hello(sibling)
    hello(z_up)
    hello(z_down)
    hello(at(x, zl, k, y, (zh + 2) % 4))
    for j in range(4):

        @pl.when(jnp.logical_not(jnp.logical_and(diagonal, x == j)))
        def _():
            hello(at(j, zl, k, x, zh))

    for rows, ref in ((0, cache_ref), (CACHE, group_ref)):
        count = ref.shape[0]
        kbuf[0, rows : rows + count, 0:RANK] = ref[:, 0:RANK]
        rope = ref[:, RANK:]
        kbuf[0, rows : rows + count, RANK:KW] = jnp.concatenate([rope, rope], axis=1)
    qbuf[0] = q_ref[...]

    pl.semaphore_wait(barrier, jnp.where(diagonal, 13, 14))

    q_copies = {}
    for d in (1, 3, 2):
        q_copies[d] = remote(
            q_ref, qbuf.at[d], sem_q, d, at((x + 4 - d) % 4, zl, k, y, zh)
        )
    half = KEYS // 2
    k_up = remote(
        kbuf.at[0, 0:half], kbuf.at[1, 0:half], sem_k, 0, z_up
    )
    k_down = remote(
        kbuf.at[0, half:KEYS], kbuf.at[1, half:KEYS], sem_k, 1, z_down
    )
    k_sib = remote(
        kbuf.at[0, 0:KEYS], kbuf.at[0, KEYS : 2 * KEYS], sem_k, 2, sibling
    )
    f_up = remote(
        kbuf.at[1, 0:half], kbuf.at[1, KEYS : KEYS + half], sem_k, 3, sibling
    )
    f_down = remote(
        kbuf.at[1, half:KEYS], kbuf.at[1, KEYS + half : 2 * KEYS], sem_k, 4, sibling
    )
    k_sib.start()
    q_copies[1].start()
    q_copies[3].start()
    k_up.start()
    k_down.start()
    q_copies[2].start()

    w_copies = [
        remote(wo_ref, wbuf.at[d], sem_w, d, at(x, zl, k, (y + 4 - d) % 4, zh))
        for d in (1, 3, 2)
    ]
    w_own = pltpu.make_async_copy(wo_ref, wbuf.at[0], sem_w.at[0, 0])
    for copy in w_copies:
        copy.start()
    w_own.start()
    mine = pl.ds(pl.multiple_of(k * HALF, 128), HALF)
    other = pl.ds(pl.multiple_of((1 - k) * HALF, 128), HALF)
    gu_remote = []
    gu_local = []
    for i, ref in enumerate((wg_ref, wu_ref)):
        lanes = pl.ds(i * HALF, HALF)
        gu_remote.append(
            remote(ref.at[0, :, other], gubuf.at[1, :, lanes], sem_gu, i, sibling)
        )
        gu_local.append(
            pltpu.make_async_copy(
                ref.at[0, :, mine], gubuf.at[0, :, lanes], sem_gu.at[0, 2 + i]
            )
        )
    wd_copy = pltpu.make_async_copy(wd_ref.at[0], wdbuf, sem_wd)
    for copy in gu_local + gu_remote + [wd_copy]:
        copy.start()

    lane = lax.broadcasted_iota(jnp.int32, (TOK, 128), 1)
    row = lax.broadcasted_iota(jnp.int32, (TOK, 128), 0)
    ahead = lane - row
    ahead2 = jnp.concatenate([ahead, ahead], axis=0)

    def scores(d, pair, side):
        queries = qabuf[d, pair * 256 : pair * 256 + 256, :]
        s = (
            lax.dot_general(
                queries,
                kbuf[side],
                (((1,), (1,)), ((), ())),
                preferred_element_type=F32,
            )
            * SCALE
        )
        token_block = 4 * ((x + d) % 4) + 2 * zl + k
        zl_key = zl if side == 0 else 1 - zl
        parts = []
        for slot in range(2):
            k_key = k if slot == 0 else 1 - k
            key_block = 4 * x + 2 * zl_key + k_key
            base = slot * KEYS
            parts.append(s[:, base : base + CACHE])
            parts.append(
                jnp.where(
                    ahead2 <= (token_block - key_block) * TOK,
                    s[:, base + CACHE : base + KEYS],
                    -1e30,
                )
            )
        return jnp.concatenate(parts, axis=1)

    def first_half(i, carry):
        d = i ^ (i // 2)

        @pl.when(i > 0)
        def _():
            remote(q_ref, qbuf.at[d], sem_q, d, sibling).wait_recv()

        for h in range(HEADS):
            lowered = mm(qbuf[d, h], wk_ref[h]).astype(BF16)
            tile = qbuf[d, HEADS + h // 2]
            keep = lane < 64 if h % 2 == 0 else lane >= 64
            qabuf[d, h * TOK : (h + 1) * TOK, 0:RANK] = lowered
            qabuf[d, h * TOK : (h + 1) * TOK, RANK:KW] = jnp.where(
                keep, tile, jnp.zeros_like(tile)
            )

        @pl.when(i == 0)
        def _():
            k_sib.wait_recv()

        for pair in range(2):
            rows = slice(pair * 256, pair * 256 + 256)
            s = scores(d, pair, 0)
            m = jnp.max(s, axis=1, keepdims=True)
            p = jnp.exp2(s - m)
            mbuf[d, rows, :] = m
            lbuf[d, rows, :] = jnp.sum(p, axis=1, keepdims=True)
            acc[d, rows, :] = mm(p.astype(BF16), kbuf[0, :, 0:RANK])

        @pl.when(i == 1)
        def _():
            k_up.wait_recv()
            f_up.start()
            k_down.wait_recv()
            f_down.start()

        return carry

    lax.fori_loop(0, 4, first_half, 0)
    f_up.wait_recv()
    f_down.wait_recv()

    def o_copies(d):
        token_x = (x + d) % 4
        device = at(y, zl, k, token_x, zh)
        return (
            remote(osend.at[d], orecv.at[x], sem_o, x, device),
            remote(ssend.at[d], srecv.at[x], sem_s, x, device),
        )

    def o_local(d):
        return (
            pltpu.make_async_copy(osend.at[d], orecv.at[x], sem_o.at[1, x]),
            pltpu.make_async_copy(ssend.at[d], srecv.at[x], sem_s.at[1, x]),
        )

    def second_half(i, carry):
        d = i ^ (i // 2)
        stats = jnp.zeros((TOK, 128), F32)
        for pair in range(2):
            rows = slice(pair * 256, pair * 256 + 256)
            s = scores(d, pair, 1)
            m_old = mbuf[d, rows, :]
            m = jnp.maximum(m_old, jnp.max(s, axis=1, keepdims=True))
            p = jnp.exp2(s - m)
            decay = jnp.exp2(m_old - m)
            total = lbuf[d, rows, :] * decay + jnp.sum(p, axis=1, keepdims=True)
            numerator = acc[d, rows, :] * decay + mm(
                p.astype(BF16), kbuf[1, :, 0:RANK]
            )
            context = (numerator / total).astype(BF16)
            lse = m + jnp.log2(total)
            for j in range(2):
                h = pair * 2 + j
                part = slice(j * TOK, (j + 1) * TOK)
                osend[d, :, h * VD : (h + 1) * VD] = mm(
                    context[part], wv_ref[h]
                ).astype(BF16)
                stats = jnp.where(lane == h, lse[part], stats)
        ssend[d] = stats.T[0:8]
        on_self = jnp.logical_and(diagonal, i == 0)

        @pl.when(on_self)
        def _():
            for copy in o_local(d):
                copy.start()

        @pl.when(jnp.logical_not(on_self))
        def _():
            for copy in o_copies(d):
                copy.start()

        return carry

    lax.fori_loop(0, 4, second_half, 0)

    for j in range(4):
        pltpu.make_async_copy(osend.at[0], orecv.at[j], sem_o.at[1, j]).wait()
        pltpu.make_async_copy(ssend.at[0], srecv.at[j], sem_s.at[1, j]).wait()
    lses = [srecv[j] for j in range(4)]
    top = jnp.maximum(jnp.maximum(lses[0], lses[1]), jnp.maximum(lses[2], lses[3]))
    shares = [jnp.exp2(lse - top) for lse in lses]
    whole = shares[0] + shares[1] + shares[2] + shares[3]
    shares = [share / whole for share in shares]
    weights = jnp.concatenate(shares + [jnp.zeros((96, 128), F32)], axis=0).T
    for h in range(HEADS):
        lanes = slice(h * VD, (h + 1) * VD)
        merged = jnp.zeros((TOK, VD), F32)
        for j in range(4):
            merged += weights[:, 8 * j + h : 8 * j + h + 1] * orecv[
                j, :, lanes
            ].astype(F32)
        agbuf[c, :, lanes] = merged.astype(BF16)

    chips = [(0, 1), (1, 0), (3, 0), (1, 1), (3, 1), (2, 0), (2, 1)]

    def ag_source(dx, dz):
        return ((x + 4 - dx) % 4) * 4 + ((zl + dz) % 2) * 2 + k

    ag_copies = []
    for i, (dx, dz) in enumerate(chips):
        copy = remote(
            agbuf.at[c],
            agbuf.at[c],
            sem_ag,
            i,
            at((x + dx) % 4, (zl + dz) % 2, k, y, zh),
        )
        copy.start()
        ag_copies.append(copy)
    forwards = [remote(agbuf.at[c], agbuf.at[c], sem_f, 7, sibling)]
    forwards[0].start()
    for i, (dx, dz) in enumerate(chips):
        source = ag_source(dx, dz)
        remote(agbuf.at[source], agbuf.at[source], sem_ag, i, sibling).wait_recv()
        copy = remote(agbuf.at[source], agbuf.at[source], sem_f, i, sibling)
        copy.start()
        forwards.append(copy)
    for i, (dx, dz) in enumerate(chips):
        source = ag_source(dx, dz) + 1 - 2 * k
        remote(agbuf.at[source], agbuf.at[source], sem_f, i, sibling).wait_recv()
    source = c + 1 - 2 * k
    remote(agbuf.at[source], agbuf.at[source], sem_f, 7, sibling).wait_recv()

    for copy in w_copies:
        copy.wait_recv()
    w_own.wait()

    def project(j):
        total = jnp.zeros((TOK, WIDTH), F32)
        for dy in range(4):
            total += mm(agbuf[4 * ((y + dy) % 4) + j], wbuf[dy])
        return total

    rs_copies = []
    for i, d in enumerate((2, 1, 3)):
        j = (zh + d) % 4
        rsend[i] = project(j).astype(BF16)
        copy = remote(rsend.at[i], rrecv.at[i], sem_rs, i, at(x, zl, k, y, j))
        copy.start()
        rs_copies.append(copy)
    total = project(zh) + res_ref[...].astype(F32)

    expert = jnp.broadcast_to(rt_ref[...], (TOK, TOK))
    expert_row = jnp.sum(
        jnp.where(lane == row, expert, 0), axis=0, keepdims=True
    )
    earlier = jnp.sum(
        jnp.where(jnp.logical_and(expert == expert_row, row < lane), 1, 0),
        axis=0,
        keepdims=True,
    )
    target = expert_row * CAP + earlier
    slots = lax.broadcasted_iota(jnp.int32, (2 * TOK, TOK), 0)
    select = jnp.where(slots == target, 1.0, 0.0).astype(BF16)

    for copy in rs_copies:
        copy.wait_recv()
    for i in range(3):
        total += rrecv[i].astype(F32)
    state[...] = total

    squares = jnp.sum(total * total, axis=1, keepdims=True)
    high = squares.astype(BF16)
    rest = squares - high.astype(F32)
    middle = rest.astype(BF16)
    low = (rest - middle.astype(F32)).astype(BF16)
    pairs = (total * gain_ref[...]).astype(BF16)
    terms = jnp.where(
        lane == 0,
        high.astype(F32),
        jnp.where(
            lane == 1, middle.astype(F32), jnp.where(lane == 2, low.astype(F32), 0.0)
        ),
    ).astype(BF16)
    dsend[:, 0:WIDTH] = mm(select, pairs).astype(BF16)
    dsend[:, 512:640] = mm(select, terms).astype(BF16)
    experts = [(dy, dz) for dy in range(4) for dz in range(4)][1:]
    d_copies = []
    for i, (dy, dz) in enumerate(experts):
        peer = 4 * ((y + dy) % 4) + (zh + dz) % 4
        copy = remote(
            dsend.at[pl.ds(peer * CAP, CAP)],
            drecv.at[0, pl.ds(e * CAP, CAP)],
            sem_d,
            i,
            (c, peer),
        )
        copy.start()
        d_copies.append(copy)
    own_rows = pl.ds(pl.multiple_of(e * CAP, CAP), CAP)
    drecv[0, own_rows, :] = dsend[own_rows, :]
    for copy in d_copies:
        copy.wait_recv()
    d_forward = remote(drecv.at[0], drecv.at[1], sem_df, 0, sibling)
    d_forward.start()

    for copy in gu_local:
        copy.wait()
    for copy in gu_remote:
        copy.wait_recv()
    d_forward.wait_recv()
    rows0 = drecv[0, :, 0:WIDTH]
    rows1 = drecv[1, :, 0:WIDTH]
    for col in range(4):
        lanes = slice(col * 512, (col + 1) * 512)
        psend[:, lanes] = (
            mm(rows0, gubuf[0, :, lanes]) + mm(rows1, gubuf[1, :, lanes])
        ).astype(BF16)
    tail = drecv[0, :, 512:640].astype(F32) + drecv[1, :, 512:640].astype(F32)
    row_squares = jnp.sum(tail, axis=1, keepdims=True)
    high = row_squares.astype(BF16)
    rest = row_squares - high.astype(F32)
    middle = rest.astype(BF16)
    low = (rest - middle.astype(F32)).astype(BF16)
    lane2 = lax.broadcasted_iota(jnp.int32, (256, 128), 1)
    psend[:, FF : FF + 128] = jnp.where(
        lane2 == 0,
        high.astype(F32),
        jnp.where(
            lane2 == 1,
            middle.astype(F32),
            jnp.where(lane2 == 2, low.astype(F32), 0.0),
        ),
    ).astype(BF16)

    chip = 2 * x + zl
    order = [(2, 1), (2, 0), (1, 1), (3, 1), (1, 0), (3, 0), (0, 1)]
    p_copies = []
    for i, (dx, dz) in enumerate(order):
        px, pz = (x + dx) % 4, (zl + dz) % 2
        copy = remote(
            psend.at[pl.ds((2 * px + pz) * 32, 32)],
            precv.at[i],
            sem_p,
            i,
            at(px, pz, k, y, zh),
        )
        copy.start()
        p_copies.append(copy)
    own32 = pl.ds(pl.multiple_of(chip * 32, 32), 32)
    summed = psend[own32, :].astype(F32)
    for i in (6, 4, 5, 2, 3, 1, 0):
        p_copies[i].wait_recv()
        summed += precv[i].astype(F32)
    mean = jnp.sum(summed[:, FF : FF + 128], axis=1, keepdims=True) / D
    factor = lax.rsqrt(mean + 1e-6)
    gate = summed[:, 0:HALF] * factor
    up = summed[:, HALF:FF] * factor
    hid[0, own32, :] = (gate / (1.0 + jnp.exp(-gate)) * up).astype(BF16)

    h_copies = []
    for i, (dx, dz) in enumerate(chips):
        copy = remote(
            hid.at[0, pl.ds(chip * 32, 32)],
            hid.at[0, pl.ds(chip * 32, 32)],
            sem_h,
            i,
            at((x + dx) % 4, (zl + dz) % 2, k, y, zh),
        )
        copy.start()
        h_copies.append(copy)

    def hid_rows(index, dx, dz):
        source = 2 * ((x + 4 - dx) % 4) + (zl + dz) % 2
        return hid.at[index, pl.ds(source * 32, 32)]

    hf_copies = [remote(hid_rows(0, 0, 0), hid_rows(1, 0, 0), sem_hf, 7, sibling)]
    hf_copies[0].start()
    for i, (dx, dz) in enumerate(chips):
        remote(hid_rows(0, dx, dz), hid_rows(0, dx, dz), sem_h, i, sibling).wait_recv()
        copy = remote(hid_rows(0, dx, dz), hid_rows(1, dx, dz), sem_hf, i, sibling)
        copy.start()
        hf_copies.append(copy)
    wd_copy.wait()
    down = mm(hid[0], wdbuf[pl.ds(pl.multiple_of(k * HALF, HALF), HALF), :])
    for copy in hf_copies:
        copy.wait_recv()
    down += mm(hid[1], wdbuf[pl.ds(pl.multiple_of((1 - k) * HALF, HALF), HALF), :])
    ysend[...] = down.astype(BF16)

    y_copies = []
    for i, (dy, dz) in enumerate(experts):
        peer = 4 * ((y + dy) % 4) + (zh + dz) % 4
        copy = remote(
            ysend.at[pl.ds(peer * CAP, CAP)],
            yrecv.at[pl.ds(e * CAP, CAP)],
            sem_y,
            i,
            (c, peer),
        )
        copy.start()
        y_copies.append(copy)
    yrecv[own_rows, :] = ysend[own_rows, :]
    for copy in y_copies:
        copy.wait_recv()
    routed = lax.dot_general(
        select, yrecv[...], (((0,), (0,)), ((), ())), preferred_element_type=F32
    )
    out_ref[...] = (state[...] + routed * rw_ref[...]).astype(BF16)

    for d in (1, 2, 3):
        q_copies[d].wait_send()
    for copy in (k_up, k_down, k_sib, f_up, f_down):
        copy.wait_send()
    for copy in w_copies + gu_remote:
        copy.wait_send()
    for d in range(4):
        if d == 0:

            @pl.when(jnp.logical_not(diagonal))
            def _():
                for copy in o_copies(0):
                    copy.wait_send()

        else:
            for copy in o_copies(d):
                copy.wait_send()
    for copy in (
        ag_copies
        + forwards
        + rs_copies
        + d_copies
        + [d_forward]
        + p_copies
        + h_copies
        + hf_copies
        + y_copies
    ):
        copy.wait_send()


def per_device(
    queries,
    latent_cache,
    group_latent,
    w_absorb_k,
    value_absorb_weight,
    w_out,
    residual,
    norm_gain,
    routes,
    route_weight,
    w_gate,
    w_up,
    w_down,
):
    rope = queries[:, :, NOPE:].reshape(TOK, 2, 128)
    packed = jnp.concatenate([queries[:, :, :NOPE], rope], axis=1).transpose(1, 0, 2)
    vmem = pl.BlockSpec(memory_space=pltpu.VMEM)
    hbm = pl.BlockSpec(memory_space=pl.ANY)
    dma = pltpu.SemaphoreType.DMA
    return pl.pallas_call(
        kernel,
        out_shape=jax.ShapeDtypeStruct((TOK, WIDTH), BF16),
        in_specs=[vmem] * 5 + [hbm] + [vmem] * 4 + [hbm] * 3,
        out_specs=vmem,
        scratch_shapes=[
            pltpu.VMEM((4, 6, TOK, 128), BF16),
            pltpu.VMEM((2, 2 * KEYS, KW), BF16),
            pltpu.VMEM((4, HEADS * TOK, KW), BF16),
            pltpu.VMEM((4, HEADS * TOK, RANK), F32),
            pltpu.VMEM((4, HEADS * TOK, 1), F32),
            pltpu.VMEM((4, HEADS * TOK, 1), F32),
            pltpu.VMEM((4, TOK, HEADS * VD), BF16),
            pltpu.VMEM((4, 8, 128), F32),
            pltpu.VMEM((4, TOK, HEADS * VD), BF16),
            pltpu.VMEM((4, 8, 128), F32),
            pltpu.VMEM((16, TOK, HEADS * VD), BF16),
            pltpu.VMEM((4, HEADS * VD, WIDTH), BF16),
            pltpu.VMEM((3, TOK, WIDTH), BF16),
            pltpu.VMEM((3, TOK, WIDTH), BF16),
            pltpu.VMEM((TOK, WIDTH), F32),
            pltpu.VMEM((2 * TOK, 640), BF16),
            pltpu.VMEM((2, 2 * TOK, 640), BF16),
            pltpu.VMEM((2, WIDTH, FF), BF16),
            pltpu.VMEM((FF, WIDTH), BF16),
            pltpu.VMEM((2 * TOK, FF + 128), BF16),
            pltpu.VMEM((7, 32, FF + 128), BF16),
            pltpu.VMEM((2, 2 * TOK, HALF), BF16),
            pltpu.VMEM((2 * TOK, WIDTH), BF16),
            pltpu.VMEM((2 * TOK, WIDTH), BF16),
            dma((2, 4)),
            dma((2, 5)),
            dma((2, 4)),
            dma((2, 4)),
            dma,
            dma((2, 4)),
            dma((2, 4)),
            dma((2, 7)),
            dma((2, 8)),
            dma((2, 3)),
            dma((2, 15)),
            dma((2, 1)),
            dma((2, 7)),
            dma((2, 7)),
            dma((2, 8)),
            dma((2, 15)),
        ],
        compiler_params=pltpu.CompilerParams(
            collective_id=0, has_side_effects=True, vmem_limit_bytes=56 * 2**20
        ),
        name="layer",
    )(
        packed,
        latent_cache,
        group_latent,
        w_absorb_k,
        value_absorb_weight,
        w_out,
        residual,
        norm_gain.reshape(1, WIDTH),
        routes,
        route_weight,
        w_gate,
        w_up,
        w_down,
    )


def solution(mesh):
    in_specs = (
        P("ctx", "exp", None),
        P("ctx", None),
        P("ctx", None),
        P("exp", None, None),
        P("exp", None, None),
        P("exp", "ctx"),
        P("exp", "ctx"),
        P("ctx"),
        P("exp", None),
        P("exp", None),
        P("exp", "ctx", None),
        P("exp", "ctx", None),
        P("exp", None, "ctx"),
    )
    out_specs = P("exp", "ctx")
    return jax.shard_map(
        per_device, mesh=mesh, in_specs=in_specs, out_specs=out_specs, check_vma=False
    )
```

```python
import math

import jax
import jax.numpy as jnp
from jax import lax
from jax.experimental import pallas as pl
from jax.experimental.pallas import tpu as pltpu
from jax.sharding import PartitionSpec as P

MESH = pl.DeviceIdType.MESH
F32 = jnp.float32
BF16 = jnp.bfloat16
D = 7168
CAP = 16
HEADS = 4
TOK = 128
NOPE = 128
RANK = 512
VD = 128
WIDTH = 448
FF = 2048
HALF = FF // 2
CACHE = 256
GROUP = 128
KEYS = CACHE + GROUP
KW = RANK + 128
SCALE = 1.0 / math.sqrt(192.0) * math.log2(math.e)


def mm(a, b):
    return jnp.dot(a, b, preferred_element_type=F32)


def mm_t(a, b):
    return lax.dot_general(a, b, (((1,), (1,)), ((), ())), preferred_element_type=F32)


def kernel(
    q_ref,
    cache_ref,
    group_ref,
    wk_ref,
    wv_ref,
    wo_ref,
    res_ref,
    gain_ref,
    rt_ref,
    rw_ref,
    wg_ref,
    wu_ref,
    wd_ref,
    out_ref,
    qbuf,
    kbuf,
    qabuf,
    acc,
    mbuf,
    lbuf,
    osend,
    ssend,
    orecv,
    srecv,
    agbuf,
    wbuf,
    product,
    rsend,
    rrecv,
    state,
    pairs,
    dsend,
    drecv,
    gubuf,
    wdbuf,
    psend,
    precv,
    hid,
    ysend,
    yrecv,
    sem_q,
    sem_k,
    sem_w,
    sem_gu,
    sem_wd,
    sem_o,
    sem_s,
    sem_ag,
    sem_f,
    sem_rs,
    sem_d,
    sem_df,
    sem_p,
    sem_h,
    sem_hf,
    sem_y,
):
    c = lax.axis_index("ctx")
    e = lax.axis_index("exp")
    x, zl, k = c // 4, (c // 2) % 2, c % 2
    y, zh = e // 4, e % 4
    z = 2 * zh + zl

    def at(x_, zl_, k_, y_, zh_):
        return (x_ * 4 + zl_ * 2 + k_, y_ * 4 + zh_)

    def at_z(z_):
        return at(x, z_ % 2, k, y, z_ // 2)

    def aligned(start, size):
        return pl.ds(pl.multiple_of(start, size), size)

    sibling = at(x, zl, 1 - k, y, zh)
    z_up = at_z((z + 1) % 8)
    z_down = at_z((z + 7) % 8)
    fixed = x == (2 * y) % 4

    def remote(src, dst, sems, i, device, j=None):
        return pltpu.make_async_remote_copy(
            src_ref=src,
            dst_ref=dst,
            send_sem=sems.at[0, i],
            recv_sem=sems.at[1, i if j is None else j],
            device_id=device,
            device_id_type=MESH,
        )

    barrier = pltpu.get_barrier_semaphore()

    def hello(device):
        pl.semaphore_signal(barrier, inc=1, device_id=device, device_id_type=MESH)

    hello(at(x, zl, k, y, (zh + 2) % 4))
    for d in (2, 1, 3):
        hello(at((x + d) % 4, zl, k, y, zh))
        hello(at(x, zl, k, (y + d) % 4, zh))
    for j in range(4):

        @pl.when(jnp.logical_not(jnp.logical_and(fixed, x == j)))
        def _():
            hello(at(j, zl, k, (x + 4 - y) % 4, zh))

    hello(z_up)
    hello(z_down)
    hello(sibling)

    kbuf[0, 0 : RANK + 64, 0:CACHE] = cache_ref[...]
    kbuf[0, RANK + 64 : KW, 0:CACHE] = cache_ref[RANK:, :]
    kbuf[0, 0 : RANK + 64, CACHE:KEYS] = group_ref[...]
    kbuf[0, RANK + 64 : KW, CACHE:KEYS] = group_ref[RANK:, :]
    for h in range(HEADS):
        qbuf[0, h] = q_ref[h, 0:NOPE, :].T
    for h in range(0, HEADS, 2):
        qbuf[0, HEADS + h // 2] = jnp.concatenate(
            [q_ref[h, NOPE:, :], q_ref[h + 1, NOPE:, :]], axis=0
        ).T

    pl.semaphore_wait(barrier, jnp.where(fixed, 13, 14))

    q_copies = {}
    for d in (1, 3, 2):
        q_copies[d] = remote(
            qbuf.at[0], qbuf.at[d], sem_q, d, at((x + 4 - d) % 4, zl, k, y, zh)
        )
    first, second = slice(0, KW // 2), slice(KW // 2, KW)
    own, others = slice(0, KEYS), slice(KEYS, 2 * KEYS)
    k_up = remote(kbuf.at[0, first, own], kbuf.at[1, first, own], sem_k, 0, z_up)
    k_down = remote(kbuf.at[0, second, own], kbuf.at[1, second, own], sem_k, 1, z_down)
    k_sib = remote(kbuf.at[0, :, own], kbuf.at[0, :, others], sem_k, 2, sibling)
    f_up = remote(kbuf.at[1, first, own], kbuf.at[1, first, others], sem_k, 3, sibling)
    f_down = remote(
        kbuf.at[1, second, own], kbuf.at[1, second, others], sem_k, 4, sibling
    )
    k_sib.start()
    q_copies[1].start()
    q_copies[3].start()
    k_up.start()
    k_down.start()
    q_copies[2].start()

    w_copies = [
        remote(wo_ref, wbuf.at[d], sem_w, d, at(x, zl, k, (y + 4 - d) % 4, zh))
        for d in (1, 3, 2)
    ]
    w_own = pltpu.make_async_copy(wo_ref, wbuf.at[0], sem_w.at[0, 0])
    w_copies[0].start()
    w_copies[1].start()
    w_own.start()
    mine, other = aligned(k * HALF, HALF), aligned((1 - k) * HALF, HALF)
    gu_remote = []
    gu_local = []
    for i, ref in enumerate((wg_ref, wu_ref)):
        lanes = pl.ds(i * HALF, HALF)
        gu_remote.append(
            remote(ref.at[0, :, other], gubuf.at[1, :, lanes], sem_gu, i, sibling)
        )
        gu_local.append(
            pltpu.make_async_copy(
                ref.at[0, :, mine], gubuf.at[0, :, lanes], sem_gu.at[0, 2 + i]
            )
        )
    wd_copy = pltpu.make_async_copy(wd_ref.at[0], wdbuf, sem_wd)
    for copy in gu_local + gu_remote + [wd_copy]:
        copy.start()

    def w_ready():
        for copy in w_copies:
            copy.wait_recv()
        w_own.wait()

    def gu_ready():
        for copy in gu_local:
            copy.wait()
        for copy in gu_remote:
            copy.wait_recv()

    background = {"w": w_ready, "gu": gu_ready, "wd": wd_copy.wait}
    sent = [q_copies[1], q_copies[2], q_copies[3], k_up, k_down, k_sib]
    sent += w_copies + gu_remote
    state[...] = res_ref[...].astype(F32).T

    lane = lax.broadcasted_iota(jnp.int32, (TOK, 128), 1)
    row = lax.broadcasted_iota(jnp.int32, (TOK, 128), 0)
    lane2 = lax.broadcasted_iota(jnp.int32, (2 * TOK, 128), 1)
    ahead = lane2 - lax.broadcasted_iota(jnp.int32, (2 * TOK, 128), 0) % 64

    def scores(d, part, side):
        s = mm(qabuf[d, part], kbuf[side])
        token_block = 4 * ((x + d) % 4) + 2 * zl + k
        zl_key = zl if side == 0 else 1 - zl
        parts = []
        for slot in range(2):
            k_key = k if slot == 0 else 1 - k
            key_block = 4 * x + 2 * zl_key + k_key
            base = slot * KEYS
            parts.append(s[:, base : base + CACHE])
            parts.append(
                jnp.where(
                    ahead <= (token_block - key_block) * TOK + 64 * part,
                    s[:, base + CACHE : base + KEYS],
                    -1e30,
                )
            )
        return jnp.concatenate(parts, axis=1)

    def values(p, side):
        return mm_t(p.astype(BF16), kbuf[side, 0:RANK, :])

    def o_copies(d, part):
        token_x = (x + d) % 4
        device = at((token_x + y) % 4, zl, k, token_x, zh)
        i, j = part * 4 + d, part * 4 + x
        return (
            remote(osend.at[part, d], orecv.at[part, x], sem_o, i, device, j),
            remote(ssend.at[part, d], srecv.at[part, x], sem_s, i, device, j),
        )

    def on_self(d):
        return jnp.logical_and(fixed, (x + d) % 4 == y)

    def finish(d, part, numerator, total, m):
        context = (numerator / total).astype(BF16)
        lse = m + jnp.log2(total)
        stats = jnp.zeros((64, 128), F32)
        for h in range(HEADS):
            rows = slice(h * 64, (h + 1) * 64)
            osend[part, d, :, h * VD : (h + 1) * VD] = mm(
                context[rows], wv_ref[h]
            ).astype(BF16)
            stats = jnp.where(lane[0:64] == h, lse[rows], stats)
        ssend[part, d] = jnp.concatenate([stats, stats], axis=0).T[0:8]

        @pl.when(on_self(d))
        def _():
            j = part * 4 + x
            pltpu.make_async_copy(
                osend.at[part, d], orecv.at[part, x], sem_o.at[1, j]
            ).start()
            pltpu.make_async_copy(
                ssend.at[part, d], srecv.at[part, x], sem_s.at[1, j]
            ).start()

        @pl.when(jnp.logical_not(on_self(d)))
        def _():
            for copy in o_copies(d, part):
                copy.start()

    def near_keys(i, carry):
        d = i ^ (i // 2)

        @pl.when(i > 0)
        def _():
            remote(qbuf.at[0], qbuf.at[d], sem_q, d, sibling).wait_recv()

        for h in range(HEADS):
            lowered = (mm(qbuf[d, h], wk_ref[h]) * SCALE).astype(BF16)
            keep = lane < 64 if h % 2 == 0 else lane >= 64
            tile = qbuf[d, HEADS + h // 2].astype(F32) * SCALE
            tile = jnp.where(keep, tile, 0.0).astype(BF16)
            for part in range(2):
                tokens = slice(part * 64, (part + 1) * 64)
                qabuf[d, part, h * 64 : (h + 1) * 64, 0:RANK] = lowered[tokens]
                qabuf[d, part, h * 64 : (h + 1) * 64, RANK:KW] = tile[tokens]

        @pl.when(i == 0)
        def _():
            k_sib.wait_recv()

        s = scores(d, 0, 0)
        m = jnp.max(s, axis=1, keepdims=True)
        p = jnp.exp2(s - m)
        mbuf[d] = m
        lbuf[d] = jnp.sum(p, axis=1, keepdims=True)
        acc[d] = values(p, 0)

        @pl.when(i == 2)
        def _():
            k_up.wait_recv()
            f_up.start()
            k_down.wait_recv()
            f_down.start()

        return carry

    def far_keys(i, carry):
        d = i ^ (i // 2)
        s = scores(d, 0, 1)
        m_old = mbuf[d]
        m = jnp.maximum(m_old, jnp.max(s, axis=1, keepdims=True))
        p = jnp.exp2(s - m)
        decay = jnp.exp2(m_old - m)
        total = lbuf[d] * decay + jnp.sum(p, axis=1, keepdims=True)
        finish(d, 0, acc[d] * decay + values(p, 1), total, m)
        return carry

    def all_keys(i, carry):
        d = i ^ (i // 2)
        s0, s1 = scores(d, 1, 0), scores(d, 1, 1)
        m = jnp.maximum(
            jnp.max(s0, axis=1, keepdims=True), jnp.max(s1, axis=1, keepdims=True)
        )
        p0, p1 = jnp.exp2(s0 - m), jnp.exp2(s1 - m)
        total = jnp.sum(p0, axis=1, keepdims=True) + jnp.sum(p1, axis=1, keepdims=True)
        finish(d, 1, values(p0, 0) + values(p1, 1), total, m)
        return carry

    chips = [(0, 1), (1, 0), (3, 0), (1, 1), (3, 1), (2, 0), (2, 1)]

    def block(part, x_, zl_, k_):
        return agbuf.at[part, x_, aligned((2 * zl_ + k_) * 64, 64)]

    def merge(part):
        for j in range(4):
            i = part * 4 + j
            pltpu.make_async_copy(
                osend.at[part, 0], orecv.at[part, j], sem_o.at[1, i]
            ).wait()
            pltpu.make_async_copy(
                ssend.at[part, 0], srecv.at[part, j], sem_s.at[1, i]
            ).wait()
        lses = [srecv[part, j] for j in range(4)]
        top = jnp.maximum(
            jnp.maximum(lses[0], lses[1]), jnp.maximum(lses[2], lses[3])
        )
        shares = [jnp.exp2(lse - top) for lse in lses]
        whole = shares[0] + shares[1] + shares[2] + shares[3]
        shares = [share / whole for share in shares]
        weights = jnp.concatenate(shares + [jnp.zeros((96, 128), F32)], axis=0).T
        rows = aligned((2 * zl + k) * 64, 64)
        for h in range(HEADS):
            lanes = slice(h * VD, (h + 1) * VD)
            merged = jnp.zeros((64, VD), F32)
            for j in range(4):
                merged += weights[0:64, 8 * j + h : 8 * j + h + 1] * orecv[
                    part, j, :, lanes
                ].astype(F32)
            agbuf[part, x, rows, lanes] = merged.astype(BF16)
        here = block(part, x, zl, k)
        copies = [remote(here, here, sem_f, part * 8 + 7, sibling)]
        for i, (dx, dz) in enumerate(chips):
            device = at((x + dx) % 4, (zl + dz) % 2, k, y, zh)
            copies.append(remote(here, here, sem_ag, part * 7 + i, device))
        for copy in copies[1:] + copies[:1]:
            copy.start()
        return copies

    def pass_on(part):
        copies = []
        for i, (dx, dz) in enumerate(chips):
            there = block(part, (x + 4 - dx) % 4, (zl + dz) % 2, k)
            remote(there, there, sem_ag, part * 7 + i, sibling).wait_recv()
            copies.append(remote(there, there, sem_f, part * 8 + i, sibling))
            copies[-1].start()
        return copies

    def gathered(part):
        for i, (dx, dz) in enumerate(chips + [(0, 0)]):
            there = block(part, (x + 4 - dx) % 4, (zl + dz) % 2, 1 - k)
            remote(there, there, sem_f, part * 8 + i, sibling).wait_recv()

    own_tokens = aligned(zh * 64, 64)

    def project(part):
        total = mm_t(agbuf[part, (2 * y) % 4], wbuf[0])
        for dy in (1, 2, 3):
            total += mm_t(agbuf[part, (2 * y + dy) % 4], wbuf[dy])
        rsend[part] = total.astype(BF16)
        copies = []
        for i, d in enumerate((2, 1, 3)):
            j = (zh + d) % 4
            copies.append(
                remote(
                    rsend.at[part, aligned(j * 64, 64)],
                    rrecv.at[part, i],
                    sem_rs,
                    part * 3 + i,
                    at(x, zl, k, y, j),
                )
            )
            copies[-1].start()
        product[...] = total
        tokens = slice(part * 64, (part + 1) * 64)
        state[tokens, :] = state[tokens, :] + product[own_tokens, :]
        return copies

    lax.fori_loop(0, 4, near_keys, 0)
    f_up.wait_recv()
    f_down.wait_recv()
    sent += [f_up, f_down]
    lax.fori_loop(0, 4, far_keys, 0)
    lax.fori_loop(0, 2, all_keys, 0)
    w_copies[2].start()
    sent += merge(0)
    lax.fori_loop(2, 4, all_keys, 0)

    expert_row = jnp.broadcast_to(rt_ref[...], (TOK, TOK))
    expert = jnp.sum(jnp.where(lane == row, expert_row, 0), axis=1, keepdims=True)
    earlier = jnp.sum(
        jnp.where(jnp.logical_and(expert == expert_row, row < lane), 1, 0),
        axis=0,
        keepdims=True,
    )
    target = rt_ref[...] * CAP + earlier
    slots = lax.broadcasted_iota(jnp.int32, (2 * TOK, TOK), 0)
    select = jnp.where(slots == target, 1.0, 0.0).astype(BF16)

    for part in range(2):
        for d in range(4):

            @pl.when(jnp.logical_not(on_self(d)))
            def _():
                for copy in o_copies(d, part):
                    copy.wait_send()

    sent += pass_on(0)
    sent += merge(1)
    gathered(0)
    background.pop("w")()
    rs_copies = project(0)
    sent += pass_on(1)
    gathered(1)
    rs_copies += project(1)
    for copy in rs_copies:
        copy.wait_recv()
    sent += rs_copies
    added = []
    for part in range(2):
        rows = state[part * 64 : (part + 1) * 64, :]
        for i in range(3):
            rows += rrecv[part, i].astype(F32)
        added.append(rows)
    total = jnp.concatenate(added, axis=0)

    def three_terms(number, lanes, start):
        high = number.astype(BF16).astype(F32)
        rest = number - high
        middle = rest.astype(BF16).astype(F32)
        low = rest - middle
        return jnp.where(
            lanes == start,
            high,
            jnp.where(
                lanes == start + 1, middle, jnp.where(lanes == start + 2, low, 0.0)
            ),
        ).astype(BF16)

    squares = jnp.sum(total * total, axis=1, keepdims=True)
    pairs[:, 0:WIDTH] = (total * gain_ref[...]).astype(BF16)
    pairs[:, WIDTH:512] = three_terms(squares, lane, 64)[:, 64:128]
    dsend[...] = mm(select, pairs[...]).astype(BF16)
    experts = [(dy, dz) for dz in (2, 1, 3, 0) for dy in (2, 1, 3, 0)][:-1]
    d_copies = {}
    for i, (dy, dz) in enumerate(experts):
        peer = 4 * ((y + dy) % 4) + (zh + dz) % 4
        d_copies[dy, dz] = remote(
            dsend.at[aligned(peer * CAP, CAP)],
            drecv.at[0, 1 - dz % 2, aligned(e // 2 * CAP, CAP)],
            sem_d,
            i,
            (c, peer),
        )
        d_copies[dy, dz].start()
    drecv[0, 1, aligned(e // 2 * CAP, CAP), :] = dsend[aligned(e * CAP, CAP), :]
    d_forwards = []
    for part in range(2):
        for (dy, dz), copy in d_copies.items():
            if 1 - dz % 2 == part:
                copy.wait_recv()
        d_forwards.append(
            remote(drecv.at[0, part], drecv.at[1, part], sem_df, part, sibling)
        )
        d_forwards[-1].start()
    sent += list(d_copies.values()) + d_forwards

    background.pop("gu")()
    chip = 2 * x + zl
    own16 = aligned(chip * 16, 16)
    order = [(2, 1), (2, 0), (1, 1), (3, 1), (1, 0), (3, 0), (0, 1)]
    p_copies = []
    for part in range(2):
        d_forwards[part].wait_recv()
        rows0 = drecv[0, part, :, 0:WIDTH]
        rows1 = drecv[1, part, :, 0:WIDTH]
        for col in range(4):
            lanes = slice(col * 512, (col + 1) * 512)
            psend[part, :, lanes] = (
                mm(rows0, gubuf[0, :, lanes]) + mm(rows1, gubuf[1, :, lanes])
            ).astype(BF16)
        tail = drecv[0, part, :, 384:512].astype(F32) + drecv[
            1, part, :, 384:512
        ].astype(F32)
        squares = jnp.sum(jnp.where(lane >= 64, tail, 0.0), axis=1, keepdims=True)
        psend[part, :, FF : FF + 128] = three_terms(squares, lane, 0)
        for i, (dx, dz) in enumerate(order):
            px, pz = (x + dx) % 4, (zl + dz) % 2
            copy = remote(
                psend.at[part, aligned((2 * px + pz) * 16, 16)],
                precv.at[part, i],
                sem_p,
                part * 7 + i,
                at(px, pz, k, y, zh),
            )
            copy.start()
            p_copies.append(copy)
    sent += p_copies

    def hid_rows(side, part, dx, dz):
        source = 2 * ((x + 4 - dx) % 4) + (zl + dz) % 2
        return hid.at[side, part, aligned(source * 16, 16)]

    h_copies = []
    hf_copies = []
    for part in range(2):
        summed = psend[part, own16, :].astype(F32)
        for i in (6, 4, 5, 2, 3, 1, 0):
            p_copies[part * 7 + i].wait_recv()
            summed += precv[part, i].astype(F32)
        mean = jnp.sum(summed[:, FF : FF + 128], axis=1, keepdims=True) / D
        factor = lax.rsqrt(mean + 1e-6)
        gate = summed[:, 0:HALF] * factor
        up = summed[:, HALF:FF] * factor
        hid[0, part, own16, :] = (gate / (1.0 + jnp.exp(-gate)) * up).astype(BF16)
        here = hid.at[0, part, own16]
        for i, (dx, dz) in enumerate(chips):
            device = at((x + dx) % 4, (zl + dz) % 2, k, y, zh)
            h_copies.append(remote(here, here, sem_h, part * 7 + i, device))
            h_copies[-1].start()
        hf_copies.append(
            remote(here, hid.at[1, part, own16], sem_hf, part * 8 + 7, sibling)
        )
        hf_copies[-1].start()
    sent += h_copies
    background.pop("wd")()
    y_copies = []
    for part in range(2):
        copies = [hf_copies[part]]
        for i, (dx, dz) in enumerate(chips):
            there = hid_rows(0, part, dx, dz)
            remote(there, there, sem_h, part * 7 + i, sibling).wait_recv()
            copies.append(
                remote(
                    there, hid_rows(1, part, dx, dz), sem_hf, part * 8 + i, sibling
                )
            )
            copies[-1].start()
        down = mm_t(hid[0, part], wdbuf[:, mine])
        for copy in copies:
            copy.wait_recv()
        sent += copies
        down += mm_t(hid[1, part], wdbuf[:, other])
        ysend[part] = down.astype(BF16)

        for i, (dy, dz) in enumerate(experts):
            if 1 - dz % 2 == part:
                peer = 4 * ((y + dy) % 4) + (zh + dz) % 4
                copy = remote(
                    ysend.at[part, aligned(peer // 2 * CAP, CAP)],
                    yrecv.at[aligned(e * CAP, CAP)],
                    sem_y,
                    i,
                    (c, peer),
                )
                copy.start()
                y_copies.append(copy)
    yrecv[aligned(e * CAP, CAP), :] = ysend[1, aligned(e // 2 * CAP, CAP), :]
    for copy in y_copies:
        copy.wait_recv()
    sent += y_copies
    routed = lax.dot_general(
        yrecv[...], select, (((0,), (0,)), ((), ())), preferred_element_type=F32
    )
    out_ref[...] = (total.T + routed * rw_ref[...]).astype(BF16)

    for copy in sent:
        copy.wait_send()


def per_device(
    queries,
    latent_cache,
    group_latent,
    w_absorb_k,
    value_absorb_weight,
    w_out,
    residual,
    norm_gain,
    routes,
    route_weight,
    w_gate,
    w_up,
    w_down,
):
    vmem = pl.BlockSpec(memory_space=pltpu.VMEM)
    hbm = pl.BlockSpec(memory_space=pl.ANY)
    dma = pltpu.SemaphoreType.DMA
    return pl.pallas_call(
        kernel,
        out_shape=jax.ShapeDtypeStruct((WIDTH, TOK), BF16),
        in_specs=[vmem] * 5 + [hbm] + [vmem] * 4 + [hbm] * 3,
        out_specs=vmem,
        scratch_shapes=[
            pltpu.VMEM((4, 6, TOK, 128), BF16),
            pltpu.VMEM((2, KW, 2 * KEYS), BF16),
            pltpu.VMEM((4, 2, HEADS * 64, KW), BF16),
            pltpu.VMEM((4, HEADS * 64, RANK), F32),
            pltpu.VMEM((4, HEADS * 64, 1), F32),
            pltpu.VMEM((4, HEADS * 64, 1), F32),
            pltpu.VMEM((2, 4, 64, HEADS * VD), BF16),
            pltpu.VMEM((2, 4, 8, 128), F32),
            pltpu.VMEM((2, 4, 64, HEADS * VD), BF16),
            pltpu.VMEM((2, 4, 8, 128), F32),
            pltpu.VMEM((2, 4, 4 * 64, HEADS * VD), BF16),
            pltpu.VMEM((4, WIDTH, HEADS * VD), BF16),
            pltpu.VMEM((4 * 64, WIDTH), F32),
            pltpu.VMEM((2, 4 * 64, WIDTH), BF16),
            pltpu.VMEM((2, 3, 64, WIDTH), BF16),
            pltpu.VMEM((TOK, WIDTH), F32),
            pltpu.VMEM((TOK, 512), BF16),
            pltpu.VMEM((2 * TOK, 512), BF16),
            pltpu.VMEM((2, 2, TOK, 512), BF16),
            pltpu.VMEM((2, WIDTH, FF), BF16),
            pltpu.VMEM((WIDTH, FF), BF16),
            pltpu.VMEM((2, TOK, FF + 128), BF16),
            pltpu.VMEM((2, 7, 16, FF + 128), BF16),
            pltpu.VMEM((2, 2, TOK, HALF), BF16),
            pltpu.VMEM((2, TOK, WIDTH), BF16),
            pltpu.VMEM((2 * TOK, WIDTH), BF16),
            dma((2, 4)),
            dma((2, 5)),
            dma((2, 4)),
            dma((2, 4)),
            dma,
            dma((2, 8)),
            dma((2, 8)),
            dma((2, 14)),
            dma((2, 16)),
            dma((2, 6)),
            dma((2, 15)),
            dma((2, 2)),
            dma((2, 14)),
            dma((2, 14)),
            dma((2, 16)),
            dma((2, 15)),
        ],
        compiler_params=pltpu.CompilerParams(
            collective_id=0, has_side_effects=True, vmem_limit_bytes=56 * 2**20
        ),
        name="layer",
    )(
        queries.transpose(1, 2, 0),
        latent_cache.T,
        group_latent.T,
        w_absorb_k,
        value_absorb_weight,
        w_out.T,
        residual.T,
        norm_gain.reshape(1, WIDTH),
        routes.T,
        route_weight.T,
        w_gate,
        w_up,
        w_down.transpose(0, 2, 1),
    ).T


def solution(mesh):
    in_specs = (
        P("ctx", "exp", None),
        P("ctx", None),
        P("ctx", None),
        P("exp", None, None),
        P("exp", None, None),
        P("exp", "ctx"),
        P("exp", "ctx"),
        P("ctx"),
        P("exp", None),
        P("exp", None),
        P("exp", "ctx", None),
        P("exp", "ctx", None),
        P("exp", None, "ctx"),
    )
    out_specs = P("exp", "ctx")
    return jax.shard_map(
        per_device, mesh=mesh, in_specs=in_specs, out_specs=out_specs, check_vma=False
    )
```

```python
import math

import jax
import jax.numpy as jnp
from jax import lax
from jax.experimental import pallas as pl
from jax.experimental.pallas import tpu as pltpu
from jax.sharding import PartitionSpec as P

MESH = pl.DeviceIdType.MESH
F32 = jnp.float32
BF16 = jnp.bfloat16
D = 7168
CAP = 16
HEADS = 4
TOK = 128
NOPE = 128
RANK = 512
VD = 128
WIDTH = 448
FF = 2048
HALF = FF // 2
CACHE = 256
GROUP = 128
KEYS = CACHE + GROUP
KW = RANK + 128
SCALE = 1.0 / math.sqrt(192.0) * math.log2(math.e)


def mm(a, b):
    return jnp.dot(a, b, preferred_element_type=F32)


def mm_t(a, b):
    return lax.dot_general(a, b, (((1,), (1,)), ((), ())), preferred_element_type=F32)


def kernel(
    q_ref,
    cache_ref,
    group_ref,
    wk_ref,
    wv_ref,
    wo_ref,
    res_ref,
    gain_ref,
    rt_ref,
    rw_ref,
    wg_ref,
    wu_ref,
    wd_ref,
    out_ref,
    qbuf,
    kbuf,
    qabuf,
    acc,
    mbuf,
    lbuf,
    osend,
    ssend,
    orecv,
    srecv,
    agbuf,
    wbuf,
    product,
    rsend,
    rrecv,
    state,
    pairs,
    dsend,
    drecv,
    gubuf,
    wdbuf,
    psend,
    precv,
    hid,
    ysend,
    yrecv,
    sem_q,
    sem_k,
    sem_w,
    sem_gu,
    sem_wd,
    sem_o,
    sem_s,
    sem_ag,
    sem_f,
    sem_rs,
    sem_d,
    sem_df,
    sem_p,
    sem_h,
    sem_hf,
    sem_y,
):
    c = lax.axis_index("ctx")
    e = lax.axis_index("exp")
    x, zl, k = c // 4, (c // 2) % 2, c % 2
    y, zh = e // 4, e % 4
    z = 2 * zh + zl

    def at(x_, zl_, k_, y_, zh_):
        return (x_ * 4 + zl_ * 2 + k_, y_ * 4 + zh_)

    def at_z(z_):
        return at(x, z_ % 2, k, y, z_ // 2)

    def aligned(start, size):
        return pl.ds(pl.multiple_of(start, size), size)

    sibling = at(x, zl, 1 - k, y, zh)
    z_up = at_z((z + 1) % 8)
    z_down = at_z((z + 7) % 8)
    fixed = x == (2 * y) % 4

    def remote(src, dst, sems, i, device, j=None):
        return pltpu.make_async_remote_copy(
            src_ref=src,
            dst_ref=dst,
            send_sem=sems.at[0, i],
            recv_sem=sems.at[1, i if j is None else j],
            device_id=device,
            device_id_type=MESH,
        )

    barrier = pltpu.get_barrier_semaphore()

    def hello(device):
        pl.semaphore_signal(barrier, inc=1, device_id=device, device_id_type=MESH)

    hello(at(x, zl, k, y, (zh + 2) % 4))
    for d in (2, 1, 3):
        hello(at((x + d) % 4, zl, k, y, zh))
        hello(at(x, zl, k, (y + d) % 4, zh))
    for j in range(4):

        @pl.when(jnp.logical_not(jnp.logical_and(fixed, x == j)))
        def _():
            hello(at(j, zl, k, (x + 4 - y) % 4, zh))

    hello(z_up)
    hello(z_down)
    hello(sibling)

    kbuf[0, 0 : RANK + 64, 0:CACHE] = cache_ref[...]
    kbuf[0, RANK + 64 : KW, 0:CACHE] = cache_ref[RANK:, :]
    kbuf[0, 0 : RANK + 64, CACHE:KEYS] = group_ref[...]
    kbuf[0, RANK + 64 : KW, CACHE:KEYS] = group_ref[RANK:, :]
    for h in range(HEADS):
        qbuf[0, h] = q_ref[h, 0:NOPE, :].T
    for h in range(0, HEADS, 2):
        qbuf[0, HEADS + h // 2] = jnp.concatenate(
            [q_ref[h, NOPE:, :], q_ref[h + 1, NOPE:, :]], axis=0
        ).T

    pl.semaphore_wait(barrier, jnp.where(fixed, 13, 14))

    q_copies = {}
    for d in (1, 3, 2):
        q_copies[d] = remote(
            qbuf.at[0], qbuf.at[d], sem_q, d, at((x + 4 - d) % 4, zl, k, y, zh)
        )
    first, second = slice(0, KW // 2), slice(KW // 2, KW)
    own, others = slice(0, KEYS), slice(KEYS, 2 * KEYS)
    k_up = remote(kbuf.at[0, first, own], kbuf.at[1, first, own], sem_k, 0, z_up)
    k_down = remote(kbuf.at[0, second, own], kbuf.at[1, second, own], sem_k, 1, z_down)
    k_sib = remote(kbuf.at[0, :, own], kbuf.at[0, :, others], sem_k, 2, sibling)
    f_up = remote(kbuf.at[1, first, own], kbuf.at[1, first, others], sem_k, 3, sibling)
    f_down = remote(
        kbuf.at[1, second, own], kbuf.at[1, second, others], sem_k, 4, sibling
    )
    k_sib.start()
    q_copies[1].start()
    q_copies[3].start()
    k_up.start()
    k_down.start()
    q_copies[2].start()

    w_copies = [
        remote(wo_ref, wbuf.at[d], sem_w, d, at(x, zl, k, (y + 4 - d) % 4, zh))
        for d in (1, 3, 2)
    ]
    w_own = pltpu.make_async_copy(wo_ref, wbuf.at[0], sem_w.at[0, 0])
    w_copies[0].start()
    w_copies[1].start()
    w_own.start()
    mine, other = aligned(k * HALF, HALF), aligned((1 - k) * HALF, HALF)
    gu_remote = []
    gu_local = []
    for i, ref in enumerate((wg_ref, wu_ref)):
        lanes = pl.ds(i * HALF, HALF)
        gu_remote.append(
            remote(ref.at[0, :, other], gubuf.at[1, :, lanes], sem_gu, i, sibling)
        )
        gu_local.append(
            pltpu.make_async_copy(
                ref.at[0, :, mine], gubuf.at[0, :, lanes], sem_gu.at[0, 2 + i]
            )
        )
    wd_copy = pltpu.make_async_copy(wd_ref.at[0], wdbuf, sem_wd)

    def w_ready():
        for copy in w_copies:
            copy.wait_recv()
        w_own.wait()

    def gu_ready():
        for copy in gu_local:
            copy.wait()
        for copy in gu_remote:
            copy.wait_recv()

    background = {"w": w_ready, "gu": gu_ready, "wd": wd_copy.wait}
    sent = [q_copies[1], q_copies[2], q_copies[3], k_up, k_down, k_sib]
    sent += w_copies + gu_remote
    state[...] = res_ref[...].astype(F32).T

    lane = lax.broadcasted_iota(jnp.int32, (TOK, 128), 1)
    row = lax.broadcasted_iota(jnp.int32, (TOK, 128), 0)
    lane2 = lax.broadcasted_iota(jnp.int32, (2 * TOK, 128), 1)
    ahead = lane2 - lax.broadcasted_iota(jnp.int32, (2 * TOK, 128), 0) % 64

    def scores(d, part, side):
        s = mm(qabuf[d, part], kbuf[side])
        token_block = 4 * ((x + d) % 4) + 2 * zl + k
        zl_key = zl if side == 0 else 1 - zl
        parts = []
        for slot in range(2):
            k_key = k if slot == 0 else 1 - k
            key_block = 4 * x + 2 * zl_key + k_key
            base = slot * KEYS
            parts.append(s[:, base : base + CACHE])
            parts.append(
                jnp.where(
                    ahead <= (token_block - key_block) * TOK + 64 * part,
                    s[:, base + CACHE : base + KEYS],
                    -1e30,
                )
            )
        return jnp.concatenate(parts, axis=1)

    def values(p, side):
        return mm_t(p.astype(BF16), kbuf[side, 0:RANK, :])

    def o_copies(d, part):
        token_x = (x + d) % 4
        device = at((token_x + y) % 4, zl, k, token_x, zh)
        i, j = part * 4 + d, part * 4 + x
        return (
            remote(osend.at[part, d], orecv.at[part, x], sem_o, i, device, j),
            remote(ssend.at[part, d], srecv.at[part, x], sem_s, i, device, j),
        )

    def on_self(d):
        return jnp.logical_and(fixed, (x + d) % 4 == y)

    def finish(d, part, numerator, total, m):
        context = (numerator / total).astype(BF16)
        lse = m + jnp.log2(total)
        stats = jnp.zeros((64, 128), F32)
        for h in range(HEADS):
            rows = slice(h * 64, (h + 1) * 64)
            osend[part, d, :, h * VD : (h + 1) * VD] = mm(
                context[rows], wv_ref[h]
            ).astype(BF16)
            stats = jnp.where(lane[0:64] == h, lse[rows], stats)
        ssend[part, d] = jnp.concatenate([stats, stats], axis=0).T[0:8]

        @pl.when(on_self(d))
        def _():
            j = part * 4 + x
            pltpu.make_async_copy(
                osend.at[part, d], orecv.at[part, x], sem_o.at[1, j]
            ).start()
            pltpu.make_async_copy(
                ssend.at[part, d], srecv.at[part, x], sem_s.at[1, j]
            ).start()

        @pl.when(jnp.logical_not(on_self(d)))
        def _():
            for copy in o_copies(d, part):
                copy.start()

    def near_keys(i, carry):
        d = i ^ (i // 2)

        @pl.when(i > 0)
        def _():
            remote(qbuf.at[0], qbuf.at[d], sem_q, d, sibling).wait_recv()

        for h in range(HEADS):
            lowered = (mm(qbuf[d, h], wk_ref[h]) * SCALE).astype(BF16)
            keep = lane < 64 if h % 2 == 0 else lane >= 64
            tile = qbuf[d, HEADS + h // 2].astype(F32) * SCALE
            tile = jnp.where(keep, tile, 0.0).astype(BF16)
            for part in range(2):
                tokens = slice(part * 64, (part + 1) * 64)
                qabuf[d, part, h * 64 : (h + 1) * 64, 0:RANK] = lowered[tokens]
                qabuf[d, part, h * 64 : (h + 1) * 64, RANK:KW] = tile[tokens]

        @pl.when(i == 0)
        def _():
            k_sib.wait_recv()

        s = scores(d, 0, 0)
        m = jnp.max(s, axis=1, keepdims=True)
        p = jnp.exp2(s - m)
        mbuf[d] = m
        lbuf[d] = jnp.sum(p, axis=1, keepdims=True)
        acc[d] = values(p, 0)

        @pl.when(i == 2)
        def _():
            k_up.wait_recv()
            f_up.start()
            k_down.wait_recv()
            f_down.start()

        return carry

    def far_keys(i, carry):
        d = i ^ (i // 2)
        s = scores(d, 0, 1)
        m_old = mbuf[d]
        m = jnp.maximum(m_old, jnp.max(s, axis=1, keepdims=True))
        p = jnp.exp2(s - m)
        decay = jnp.exp2(m_old - m)
        total = lbuf[d] * decay + jnp.sum(p, axis=1, keepdims=True)
        finish(d, 0, acc[d] * decay + values(p, 1), total, m)
        return carry

    def all_keys(i, carry):
        d = i ^ (i // 2)
        s0, s1 = scores(d, 1, 0), scores(d, 1, 1)
        m = jnp.maximum(
            jnp.max(s0, axis=1, keepdims=True), jnp.max(s1, axis=1, keepdims=True)
        )
        p0, p1 = jnp.exp2(s0 - m), jnp.exp2(s1 - m)
        total = jnp.sum(p0, axis=1, keepdims=True) + jnp.sum(p1, axis=1, keepdims=True)
        finish(d, 1, values(p0, 0) + values(p1, 1), total, m)
        return carry

    chips = [(0, 1), (1, 0), (3, 0), (1, 1), (3, 1), (2, 0), (2, 1)]

    def block(part, x_, zl_, k_):
        return agbuf.at[part, x_, aligned((2 * zl_ + k_) * 64, 64)]

    def merge(part):
        for j in range(4):
            i = part * 4 + j
            pltpu.make_async_copy(
                osend.at[part, 0], orecv.at[part, j], sem_o.at[1, i]
            ).wait()
            pltpu.make_async_copy(
                ssend.at[part, 0], srecv.at[part, j], sem_s.at[1, i]
            ).wait()
        lses = [srecv[part, j] for j in range(4)]
        top = jnp.maximum(
            jnp.maximum(lses[0], lses[1]), jnp.maximum(lses[2], lses[3])
        )
        shares = [jnp.exp2(lse - top) for lse in lses]
        whole = shares[0] + shares[1] + shares[2] + shares[3]
        shares = [share / whole for share in shares]
        weights = jnp.concatenate(shares + [jnp.zeros((96, 128), F32)], axis=0).T
        rows = aligned((2 * zl + k) * 64, 64)
        for h in range(HEADS):
            lanes = slice(h * VD, (h + 1) * VD)
            merged = jnp.zeros((64, VD), F32)
            for j in range(4):
                merged += weights[0:64, 8 * j + h : 8 * j + h + 1] * orecv[
                    part, j, :, lanes
                ].astype(F32)
            agbuf[part, x, rows, lanes] = merged.astype(BF16)
        here = block(part, x, zl, k)
        copies = [remote(here, here, sem_f, part * 8 + 7, sibling)]
        for i, (dx, dz) in enumerate(chips):
            device = at((x + dx) % 4, (zl + dz) % 2, k, y, zh)
            copies.append(remote(here, here, sem_ag, part * 7 + i, device))
        for copy in copies[1:] + copies[:1]:
            copy.start()
        return copies

    def pass_on(part):
        copies = []
        for i, (dx, dz) in enumerate(chips):
            there = block(part, (x + 4 - dx) % 4, (zl + dz) % 2, k)
            remote(there, there, sem_ag, part * 7 + i, sibling).wait_recv()
            copies.append(remote(there, there, sem_f, part * 8 + i, sibling))
            copies[-1].start()
        return copies

    def gathered(part):
        for i, (dx, dz) in enumerate(chips + [(0, 0)]):
            there = block(part, (x + 4 - dx) % 4, (zl + dz) % 2, 1 - k)
            remote(there, there, sem_f, part * 8 + i, sibling).wait_recv()

    own_tokens = aligned(zh * 64, 64)

    def project(part):
        total = mm_t(agbuf[part, (2 * y) % 4], wbuf[0])
        for dy in (1, 2, 3):
            total += mm_t(agbuf[part, (2 * y + dy) % 4], wbuf[dy])
        rsend[part] = total.astype(BF16)
        copies = []
        for i, d in enumerate((2, 1, 3)):
            j = (zh + d) % 4
            copies.append(
                remote(
                    rsend.at[part, aligned(j * 64, 64)],
                    rrecv.at[part, i],
                    sem_rs,
                    part * 3 + i,
                    at(x, zl, k, y, j),
                )
            )
            copies[-1].start()
        product[...] = total
        tokens = slice(part * 64, (part + 1) * 64)
        state[tokens, :] = state[tokens, :] + product[own_tokens, :]
        return copies

    lax.fori_loop(0, 3, near_keys, 0)
    f_up.wait_recv()
    f_down.wait_recv()
    sent += [f_up, f_down]
    lax.fori_loop(0, 3, far_keys, 0)
    lax.fori_loop(3, 4, near_keys, 0)
    lax.fori_loop(3, 4, far_keys, 0)
    for copy in gu_local + gu_remote + [wd_copy]:
        copy.start()
    lax.fori_loop(0, 3, all_keys, 0)
    sent += merge(0)
    lax.fori_loop(3, 4, all_keys, 0)
    w_copies[2].start()

    expert_row = jnp.broadcast_to(rt_ref[...], (TOK, TOK))
    expert = jnp.sum(jnp.where(lane == row, expert_row, 0), axis=1, keepdims=True)
    earlier = jnp.sum(
        jnp.where(jnp.logical_and(expert == expert_row, row < lane), 1, 0),
        axis=0,
        keepdims=True,
    )
    target = rt_ref[...] * CAP + earlier
    slots = lax.broadcasted_iota(jnp.int32, (2 * TOK, TOK), 0)
    select = jnp.where(slots == target, 1.0, 0.0).astype(BF16)

    sent += merge(1)
    sent += pass_on(0)
    gathered(0)
    background.pop("w")()
    rs_copies = project(0)
    sent += pass_on(1)
    gathered(1)
    rs_copies += project(1)
    for copy in rs_copies:
        copy.wait_recv()
    sent += rs_copies
    added = []
    for part in range(2):
        rows = state[part * 64 : (part + 1) * 64, :]
        for i in range(3):
            rows += rrecv[part, i].astype(F32)
        added.append(rows)
    total = jnp.concatenate(added, axis=0)

    def three_terms(number, lanes, start):
        high = number.astype(BF16).astype(F32)
        rest = number - high
        middle = rest.astype(BF16).astype(F32)
        low = rest - middle
        return jnp.where(
            lanes == start,
            high,
            jnp.where(
                lanes == start + 1, middle, jnp.where(lanes == start + 2, low, 0.0)
            ),
        ).astype(BF16)

    squares = jnp.sum(total * total, axis=1, keepdims=True)
    pairs[:, 0:WIDTH] = (total * gain_ref[...]).astype(BF16)
    pairs[:, WIDTH:512] = three_terms(squares, lane, 64)[:, 64:128]
    dsend[...] = mm(select, pairs[...]).astype(BF16)
    experts = [(dy, dz) for dz in (1, 3, 2, 0) for dy in (2, 1, 3, 0)][:-1]
    d_copies = {}
    for i, (dy, dz) in enumerate(experts):
        peer = 4 * ((y + dy) % 4) + (zh + dz) % 4
        d_copies[dy, dz] = remote(
            dsend.at[aligned(peer * CAP, CAP)],
            drecv.at[0, 1 - dz % 2, aligned(e // 2 * CAP, CAP)],
            sem_d,
            i,
            (c, peer),
        )
        d_copies[dy, dz].start()
    drecv[0, 1, aligned(e // 2 * CAP, CAP), :] = dsend[aligned(e * CAP, CAP), :]
    d_forwards = []
    for part in range(2):
        for (dy, dz), copy in d_copies.items():
            if 1 - dz % 2 == part:
                copy.wait_recv()
        d_forwards.append(
            remote(drecv.at[0, part], drecv.at[1, part], sem_df, part, sibling)
        )
        d_forwards[-1].start()
    sent += list(d_copies.values()) + d_forwards

    background.pop("gu")()
    chip = 2 * x + zl
    own16 = aligned(chip * 16, 16)
    order = [(2, 1), (2, 0), (1, 1), (3, 1), (1, 0), (3, 0), (0, 1)]
    p_copies = []
    for part in range(2):
        d_forwards[part].wait_recv()
        rows0 = drecv[0, part, :, 0:WIDTH]
        rows1 = drecv[1, part, :, 0:WIDTH]
        for col in range(4):
            lanes = slice(col * 512, (col + 1) * 512)
            psend[part, :, lanes] = (
                mm(rows0, gubuf[0, :, lanes]) + mm(rows1, gubuf[1, :, lanes])
            ).astype(BF16)
        tail = drecv[0, part, :, 384:512].astype(F32) + drecv[
            1, part, :, 384:512
        ].astype(F32)
        squares = jnp.sum(jnp.where(lane >= 64, tail, 0.0), axis=1, keepdims=True)
        psend[part, :, FF : FF + 128] = three_terms(squares, lane, 0)
        for i, (dx, dz) in enumerate(order):
            px, pz = (x + dx) % 4, (zl + dz) % 2
            copy = remote(
                psend.at[part, aligned((2 * px + pz) * 16, 16)],
                precv.at[part, i],
                sem_p,
                part * 7 + i,
                at(px, pz, k, y, zh),
            )
            copy.start()
            p_copies.append(copy)
    sent += p_copies

    def hid_rows(side, part, dx, dz):
        source = 2 * ((x + 4 - dx) % 4) + (zl + dz) % 2
        return hid.at[side, part, aligned(source * 16, 16)]

    h_copies = []
    hf_copies = []
    for part in range(2):
        summed = psend[part, own16, :].astype(F32)
        for i in (6, 4, 5, 2, 3, 1, 0):
            p_copies[part * 7 + i].wait_recv()
            summed += precv[part, i].astype(F32)
        mean = jnp.sum(summed[:, FF : FF + 128], axis=1, keepdims=True) / D
        factor = lax.rsqrt(mean + 1e-6)
        gate = summed[:, 0:HALF] * factor
        up = summed[:, HALF:FF] * factor
        hid[0, part, own16, :] = (gate / (1.0 + jnp.exp(-gate)) * up).astype(BF16)
        here = hid.at[0, part, own16]
        for i, (dx, dz) in enumerate(chips):
            device = at((x + dx) % 4, (zl + dz) % 2, k, y, zh)
            h_copies.append(remote(here, here, sem_h, part * 7 + i, device))
            h_copies[-1].start()
        hf_copies.append(
            remote(here, hid.at[1, part, own16], sem_hf, part * 8 + 7, sibling)
        )
        hf_copies[-1].start()
    sent += h_copies
    background.pop("wd")()
    y_copies = []
    for part in range(2):
        copies = [hf_copies[part]]
        for i, (dx, dz) in enumerate(chips):
            there = hid_rows(0, part, dx, dz)
            remote(there, there, sem_h, part * 7 + i, sibling).wait_recv()
            copies.append(
                remote(
                    there, hid_rows(1, part, dx, dz), sem_hf, part * 8 + i, sibling
                )
            )
            copies[-1].start()
        down = mm_t(hid[0, part], wdbuf[:, mine])
        for copy in copies:
            copy.wait_recv()
        sent += copies
        down += mm_t(hid[1, part], wdbuf[:, other])
        ysend[part] = down.astype(BF16)

        for i, (dy, dz) in enumerate(experts):
            if 1 - dz % 2 == part:
                peer = 4 * ((y + dy) % 4) + (zh + dz) % 4
                copy = remote(
                    ysend.at[part, aligned(peer // 2 * CAP, CAP)],
                    yrecv.at[aligned(e * CAP, CAP)],
                    sem_y,
                    i,
                    (c, peer),
                )
                copy.start()
                y_copies.append(copy)
    yrecv[aligned(e * CAP, CAP), :] = ysend[1, aligned(e // 2 * CAP, CAP), :]
    for copy in y_copies:
        copy.wait_recv()
    sent += y_copies
    routed = lax.dot_general(
        yrecv[...], select, (((0,), (0,)), ((), ())), preferred_element_type=F32
    )
    out_ref[...] = (total.T + routed * rw_ref[...]).astype(BF16)

    for part in range(2):
        for d in range(4):

            @pl.when(jnp.logical_not(on_self(d)))
            def _():
                for copy in o_copies(d, part):
                    copy.wait_send()
    for copy in sent:
        copy.wait_send()


def per_device(
    queries,
    latent_cache,
    group_latent,
    w_absorb_k,
    value_absorb_weight,
    w_out,
    residual,
    norm_gain,
    routes,
    route_weight,
    w_gate,
    w_up,
    w_down,
):
    vmem = pl.BlockSpec(memory_space=pltpu.VMEM)
    hbm = pl.BlockSpec(memory_space=pl.ANY)
    dma = pltpu.SemaphoreType.DMA
    return pl.pallas_call(
        kernel,
        out_shape=jax.ShapeDtypeStruct((WIDTH, TOK), BF16),
        in_specs=[vmem] * 5 + [hbm] + [vmem] * 4 + [hbm] * 3,
        out_specs=vmem,
        scratch_shapes=[
            pltpu.VMEM((4, 6, TOK, 128), BF16),
            pltpu.VMEM((2, KW, 2 * KEYS), BF16),
            pltpu.VMEM((4, 2, HEADS * 64, KW), BF16),
            pltpu.VMEM((4, HEADS * 64, RANK), F32),
            pltpu.VMEM((4, HEADS * 64, 1), F32),
            pltpu.VMEM((4, HEADS * 64, 1), F32),
            pltpu.VMEM((2, 4, 64, HEADS * VD), BF16),
            pltpu.VMEM((2, 4, 8, 128), F32),
            pltpu.VMEM((2, 4, 64, HEADS * VD), BF16),
            pltpu.VMEM((2, 4, 8, 128), F32),
            pltpu.VMEM((2, 4, 4 * 64, HEADS * VD), BF16),
            pltpu.VMEM((4, WIDTH, HEADS * VD), BF16),
            pltpu.VMEM((4 * 64, WIDTH), F32),
            pltpu.VMEM((2, 4 * 64, WIDTH), BF16),
            pltpu.VMEM((2, 3, 64, WIDTH), BF16),
            pltpu.VMEM((TOK, WIDTH), F32),
            pltpu.VMEM((TOK, 512), BF16),
            pltpu.VMEM((2 * TOK, 512), BF16),
            pltpu.VMEM((2, 2, TOK, 512), BF16),
            pltpu.VMEM((2, WIDTH, FF), BF16),
            pltpu.VMEM((WIDTH, FF), BF16),
            pltpu.VMEM((2, TOK, FF + 128), BF16),
            pltpu.VMEM((2, 7, 16, FF + 128), BF16),
            pltpu.VMEM((2, 2, TOK, HALF), BF16),
            pltpu.VMEM((2, TOK, WIDTH), BF16),
            pltpu.VMEM((2 * TOK, WIDTH), BF16),
            dma((2, 4)),
            dma((2, 5)),
            dma((2, 4)),
            dma((2, 4)),
            dma,
            dma((2, 8)),
            dma((2, 8)),
            dma((2, 14)),
            dma((2, 16)),
            dma((2, 6)),
            dma((2, 15)),
            dma((2, 2)),
            dma((2, 14)),
            dma((2, 14)),
            dma((2, 16)),
            dma((2, 15)),
        ],
        compiler_params=pltpu.CompilerParams(
            collective_id=0, has_side_effects=True, vmem_limit_bytes=56 * 2**20
        ),
        name="layer",
    )(
        queries.transpose(1, 2, 0),
        latent_cache.T,
        group_latent.T,
        w_absorb_k,
        value_absorb_weight,
        w_out.T,
        residual.T,
        norm_gain.reshape(1, WIDTH),
        routes.T,
        route_weight.T,
        w_gate,
        w_up,
        w_down.transpose(0, 2, 1),
    ).T


def solution(mesh):
    in_specs = (
        P("ctx", "exp", None),
        P("ctx", None),
        P("ctx", None),
        P("exp", None, None),
        P("exp", None, None),
        P("exp", "ctx"),
        P("exp", "ctx"),
        P("ctx"),
        P("exp", None),
        P("exp", None),
        P("exp", "ctx", None),
        P("exp", "ctx", None),
        P("exp", None, "ctx"),
    )
    out_specs = P("exp", "ctx")
    return jax.shard_map(
        per_device, mesh=mesh, in_specs=in_specs, out_specs=out_specs, check_vma=False
    )
```

```python
import math

import jax
import jax.numpy as jnp
from jax import lax
from jax.experimental import pallas as pl
from jax.experimental.pallas import tpu as pltpu
from jax.sharding import PartitionSpec as P

MESH = pl.DeviceIdType.MESH
F32 = jnp.float32
BF16 = jnp.bfloat16
D = 7168
CAP = 16
HEADS = 4
TOK = 128
NOPE = 128
RANK = 512
VD = 128
WIDTH = 448
FF = 2048
HALF = FF // 2
CACHE = 256
GROUP = 128
KEYS = CACHE + GROUP
KW = RANK + 128
SCALE = 1.0 / math.sqrt(192.0) * math.log2(math.e)


def mm(a, b):
    return jnp.dot(a, b, preferred_element_type=F32)


def mm_t(a, b):
    return lax.dot_general(a, b, (((1,), (1,)), ((), ())), preferred_element_type=F32)


def kernel(
    q_ref,
    cache_ref,
    group_ref,
    wk_ref,
    wv_ref,
    wo_ref,
    res_ref,
    gain_ref,
    rt_ref,
    rw_ref,
    wg_ref,
    wu_ref,
    wd_ref,
    out_ref,
    qbuf,
    kbuf,
    qabuf,
    acc,
    mbuf,
    lbuf,
    osend,
    ssend,
    orecv,
    srecv,
    agbuf,
    wbuf,
    product,
    rsend,
    rrecv,
    state,
    pairs,
    dsend,
    drecv,
    gubuf,
    wdbuf,
    psend,
    precv,
    hid,
    ysend,
    yrecv,
    sem_q,
    sem_k,
    sem_w,
    sem_gu,
    sem_wd,
    sem_o,
    sem_s,
    sem_ag,
    sem_f,
    sem_rs,
    sem_d,
    sem_df,
    sem_p,
    sem_h,
    sem_hf,
    sem_y,
):
    c = lax.axis_index("ctx")
    e = lax.axis_index("exp")
    x, zl, k = c // 4, (c // 2) % 2, c % 2
    y, zh = e // 4, e % 4
    z = 2 * zh + zl

    def at(x_, zl_, k_, y_, zh_):
        return (x_ * 4 + zl_ * 2 + k_, y_ * 4 + zh_)

    def at_z(z_):
        return at(x, z_ % 2, k, y, z_ // 2)

    def aligned(start, size):
        return pl.ds(pl.multiple_of(start, size), size)

    sibling = at(x, zl, 1 - k, y, zh)
    z_up = at_z((z + 1) % 8)
    z_down = at_z((z + 7) % 8)
    fixed = x == (2 * y) % 4

    def remote(src, dst, sems, i, device, j=None):
        return pltpu.make_async_remote_copy(
            src_ref=src,
            dst_ref=dst,
            send_sem=sems.at[0, i],
            recv_sem=sems.at[1, i if j is None else j],
            device_id=device,
            device_id_type=MESH,
        )

    barrier = pltpu.get_barrier_semaphore()

    def hello(device):
        pl.semaphore_signal(barrier, inc=1, device_id=device, device_id_type=MESH)

    hello(at(x, zl, k, y, (zh + 2) % 4))
    for d in (2, 1, 3):
        hello(at((x + d) % 4, zl, k, y, zh))
        hello(at(x, zl, k, (y + d) % 4, zh))
    for j in range(4):

        @pl.when(jnp.logical_not(jnp.logical_and(fixed, x == j)))
        def _():
            hello(at(j, zl, k, (x + 4 - y) % 4, zh))

    hello(z_up)
    hello(z_down)
    hello(sibling)

    kbuf[0, 0 : RANK + 64, 0:CACHE] = cache_ref[...]
    kbuf[0, RANK + 64 : KW, 0:CACHE] = cache_ref[RANK:, :]
    kbuf[0, 0 : RANK + 64, CACHE:KEYS] = group_ref[...]
    kbuf[0, RANK + 64 : KW, CACHE:KEYS] = group_ref[RANK:, :]
    for h in range(HEADS):
        qbuf[0, h] = q_ref[h, 0:NOPE, :].T
    for h in range(0, HEADS, 2):
        qbuf[0, HEADS + h // 2] = jnp.concatenate(
            [q_ref[h, NOPE:, :], q_ref[h + 1, NOPE:, :]], axis=0
        ).T

    pl.semaphore_wait(barrier, jnp.where(fixed, 13, 14))

    q_copies = {}
    for d in (1, 3, 2):
        q_copies[d] = remote(
            qbuf.at[0], qbuf.at[d], sem_q, d, at((x + 4 - d) % 4, zl, k, y, zh)
        )
    first, second = slice(0, KW // 2), slice(KW // 2, KW)
    own, others = slice(0, KEYS), slice(KEYS, 2 * KEYS)
    k_up = remote(kbuf.at[0, first, own], kbuf.at[1, first, own], sem_k, 0, z_up)
    k_down = remote(kbuf.at[0, second, own], kbuf.at[1, second, own], sem_k, 1, z_down)
    k_sib = remote(kbuf.at[0, :, own], kbuf.at[0, :, others], sem_k, 2, sibling)
    f_up = remote(kbuf.at[1, first, own], kbuf.at[1, first, others], sem_k, 3, sibling)
    f_down = remote(
        kbuf.at[1, second, own], kbuf.at[1, second, others], sem_k, 4, sibling
    )
    k_sib.start()
    q_copies[1].start()
    q_copies[3].start()
    k_up.start()
    k_down.start()
    q_copies[2].start()

    w_copies = [
        remote(wo_ref, wbuf.at[d], sem_w, d, at(x, zl, k, (y + 4 - d) % 4, zh))
        for d in (1, 3, 2)
    ]
    w_own = pltpu.make_async_copy(wo_ref, wbuf.at[0], sem_w.at[0, 0])
    w_copies[0].start()
    w_copies[1].start()
    w_own.start()
    mine, other = aligned(k * HALF, HALF), aligned((1 - k) * HALF, HALF)
    gu_remote = []
    gu_local = []
    for i, ref in enumerate((wg_ref, wu_ref)):
        lanes = pl.ds(i * HALF, HALF)
        gu_remote.append(
            remote(ref.at[0, :, other], gubuf.at[1, :, lanes], sem_gu, i, sibling)
        )
        gu_local.append(
            pltpu.make_async_copy(
                ref.at[0, :, mine], gubuf.at[0, :, lanes], sem_gu.at[0, 2 + i]
            )
        )
    wd_copy = pltpu.make_async_copy(wd_ref.at[0], wdbuf, sem_wd)

    def w_ready():
        for copy in w_copies:
            copy.wait_recv()
        w_own.wait()

    def gu_ready():
        for copy in gu_local:
            copy.wait()
        for copy in gu_remote:
            copy.wait_recv()

    background = {"w": w_ready, "gu": gu_ready, "wd": wd_copy.wait}
    sent = [q_copies[1], q_copies[2], q_copies[3], k_up, k_down, k_sib]
    sent += w_copies + gu_remote
    state[...] = res_ref[...].astype(F32).T

    lane = lax.broadcasted_iota(jnp.int32, (TOK, 128), 1)
    row = lax.broadcasted_iota(jnp.int32, (TOK, 128), 0)
    lane2 = lax.broadcasted_iota(jnp.int32, (2 * TOK, 128), 1)
    ahead = lane2 - lax.broadcasted_iota(jnp.int32, (2 * TOK, 128), 0) % 64

    def scores(d, part, side):
        s = mm(qabuf[d, part], kbuf[side])
        token_block = 4 * ((x + d) % 4) + 2 * zl + k
        zl_key = zl if side == 0 else 1 - zl
        parts = []
        for slot in range(2):
            k_key = k if slot == 0 else 1 - k
            key_block = 4 * x + 2 * zl_key + k_key
            base = slot * KEYS
            parts.append(s[:, base : base + CACHE])
            parts.append(
                jnp.where(
                    ahead <= (token_block - key_block) * TOK + 64 * part,
                    s[:, base + CACHE : base + KEYS],
                    -1e30,
                )
            )
        return jnp.concatenate(parts, axis=1)

    def values(p, side):
        return mm_t(p.astype(BF16), kbuf[side, 0:RANK, :])

    def o_copies(d, part):
        token_x = (x + d) % 4
        device = at((token_x + y) % 4, zl, k, token_x, zh)
        i, j = part * 4 + d, part * 4 + x
        return (
            remote(osend.at[part, d], orecv.at[part, x], sem_o, i, device, j),
            remote(ssend.at[part, d], srecv.at[part, x], sem_s, i, device, j),
        )

    def on_self(d):
        return jnp.logical_and(fixed, (x + d) % 4 == y)

    def finish(d, part, numerator, total, m):
        context = (numerator / total).astype(BF16)
        lse = m + jnp.log2(total)
        stats = jnp.zeros((64, 128), F32)
        for h in range(HEADS):
            rows = slice(h * 64, (h + 1) * 64)
            osend[part, d, :, h * VD : (h + 1) * VD] = mm(
                context[rows], wv_ref[h]
            ).astype(BF16)
            stats = jnp.where(lane[0:64] == h, lse[rows], stats)
        ssend[part, d] = jnp.concatenate([stats, stats], axis=0).T[0:8]

        @pl.when(on_self(d))
        def _():
            j = part * 4 + x
            pltpu.make_async_copy(
                osend.at[part, d], orecv.at[part, x], sem_o.at[1, j]
            ).start()
            pltpu.make_async_copy(
                ssend.at[part, d], srecv.at[part, x], sem_s.at[1, j]
            ).start()

        @pl.when(jnp.logical_not(on_self(d)))
        def _():
            for copy in o_copies(d, part):
                copy.start()

    def near_keys(i, carry):
        d = i ^ (i // 2)

        @pl.when(i > 0)
        def _():
            remote(qbuf.at[0], qbuf.at[d], sem_q, d, sibling).wait_recv()

        for h in range(HEADS):
            lowered = (mm(qbuf[d, h], wk_ref[h]) * SCALE).astype(BF16)
            keep = lane < 64 if h % 2 == 0 else lane >= 64
            tile = qbuf[d, HEADS + h // 2].astype(F32) * SCALE
            tile = jnp.where(keep, tile, 0.0).astype(BF16)
            for part in range(2):
                tokens = slice(part * 64, (part + 1) * 64)
                qabuf[d, part, h * 64 : (h + 1) * 64, 0:RANK] = lowered[tokens]
                qabuf[d, part, h * 64 : (h + 1) * 64, RANK:KW] = tile[tokens]

        @pl.when(i == 0)
        def _():
            k_sib.wait_recv()

        s = scores(d, 0, 0)
        m = jnp.max(s, axis=1, keepdims=True)
        p = jnp.exp2(s - m)
        mbuf[d] = m
        lbuf[d] = jnp.sum(p, axis=1, keepdims=True)
        acc[d] = values(p, 0)

        @pl.when(i == 2)
        def _():
            k_up.wait_recv()
            f_up.start()
            k_down.wait_recv()
            f_down.start()

        return carry

    def far_keys(i, carry):
        d = i ^ (i // 2)
        s = scores(d, 0, 1)
        m_old = mbuf[d]
        m = jnp.maximum(m_old, jnp.max(s, axis=1, keepdims=True))
        p = jnp.exp2(s - m)
        decay = jnp.exp2(m_old - m)
        total = lbuf[d] * decay + jnp.sum(p, axis=1, keepdims=True)
        finish(d, 0, acc[d] * decay + values(p, 1), total, m)
        return carry

    def all_keys(i, carry):
        d = i ^ (i // 2)
        s0, s1 = scores(d, 1, 0), scores(d, 1, 1)
        m = jnp.maximum(
            jnp.max(s0, axis=1, keepdims=True), jnp.max(s1, axis=1, keepdims=True)
        )
        p0, p1 = jnp.exp2(s0 - m), jnp.exp2(s1 - m)
        total = jnp.sum(p0, axis=1, keepdims=True) + jnp.sum(p1, axis=1, keepdims=True)
        finish(d, 1, values(p0, 0) + values(p1, 1), total, m)
        return carry

    chips = [(0, 1), (1, 0), (3, 0), (1, 1), (3, 1), (2, 0), (2, 1)]

    def block(part, x_, zl_, k_):
        return agbuf.at[part, x_, aligned((2 * zl_ + k_) * 64, 64)]

    def merge(part):
        for j in range(4):
            i = part * 4 + j
            pltpu.make_async_copy(
                osend.at[part, 0], orecv.at[part, j], sem_o.at[1, i]
            ).wait()
            pltpu.make_async_copy(
                ssend.at[part, 0], srecv.at[part, j], sem_s.at[1, i]
            ).wait()
        lses = [srecv[part, j] for j in range(4)]
        top = jnp.maximum(
            jnp.maximum(lses[0], lses[1]), jnp.maximum(lses[2], lses[3])
        )
        shares = [jnp.exp2(lse - top) for lse in lses]
        whole = shares[0] + shares[1] + shares[2] + shares[3]
        shares = [share / whole for share in shares]
        weights = jnp.concatenate(shares + [jnp.zeros((96, 128), F32)], axis=0).T
        rows = aligned((2 * zl + k) * 64, 64)
        for h in range(HEADS):
            lanes = slice(h * VD, (h + 1) * VD)
            merged = jnp.zeros((64, VD), F32)
            for j in range(4):
                merged += weights[0:64, 8 * j + h : 8 * j + h + 1] * orecv[
                    part, j, :, lanes
                ].astype(F32)
            agbuf[part, x, rows, lanes] = merged.astype(BF16)
        here = block(part, x, zl, k)
        copies = [remote(here, here, sem_f, part * 8 + 7, sibling)]
        for i, (dx, dz) in enumerate(chips):
            device = at((x + dx) % 4, (zl + dz) % 2, k, y, zh)
            copies.append(remote(here, here, sem_ag, part * 7 + i, device))
        for copy in copies[1:] + copies[:1]:
            copy.start()
        return copies

    def pass_on(part):
        copies = []
        for i, (dx, dz) in enumerate(chips):
            there = block(part, (x + 4 - dx) % 4, (zl + dz) % 2, k)
            remote(there, there, sem_ag, part * 7 + i, sibling).wait_recv()
            copies.append(remote(there, there, sem_f, part * 8 + i, sibling))
            copies[-1].start()
        return copies

    def gathered(part):
        for i, (dx, dz) in enumerate(chips + [(0, 0)]):
            there = block(part, (x + 4 - dx) % 4, (zl + dz) % 2, 1 - k)
            remote(there, there, sem_f, part * 8 + i, sibling).wait_recv()

    own_tokens = aligned(zh * 64, 64)

    def project(part):
        total = mm_t(agbuf[part, (2 * y) % 4], wbuf[0])
        for dy in (1, 2, 3):
            total += mm_t(agbuf[part, (2 * y + dy) % 4], wbuf[dy])
        rsend[part] = total.astype(BF16)
        copies = []
        for i, d in enumerate((2, 1, 3)):
            j = (zh + d) % 4
            copies.append(
                remote(
                    rsend.at[part, aligned(j * 64, 64)],
                    rrecv.at[part, i],
                    sem_rs,
                    part * 3 + i,
                    at(x, zl, k, y, j),
                )
            )
            copies[-1].start()
        product[...] = total
        tokens = slice(part * 64, (part + 1) * 64)
        state[tokens, :] = state[tokens, :] + product[own_tokens, :]
        return copies

    lax.fori_loop(0, 3, near_keys, 0)
    f_up.wait_recv()
    f_down.wait_recv()
    sent += [f_up, f_down]
    lax.fori_loop(0, 3, far_keys, 0, unroll=3)
    lax.fori_loop(3, 4, near_keys, 0)
    lax.fori_loop(3, 4, far_keys, 0)
    for copy in gu_local + gu_remote + [wd_copy]:
        copy.start()
    lax.fori_loop(0, 2, all_keys, 0, unroll=2)
    sent += merge(0)
    lax.fori_loop(2, 4, all_keys, 0, unroll=2)
    w_copies[2].start()

    expert_row = jnp.broadcast_to(rt_ref[...], (TOK, TOK))
    expert = jnp.sum(jnp.where(lane == row, expert_row, 0), axis=1, keepdims=True)
    earlier = jnp.sum(
        jnp.where(jnp.logical_and(expert == expert_row, row < lane), 1, 0),
        axis=0,
        keepdims=True,
    )
    target = rt_ref[...] * CAP + earlier
    slots = lax.broadcasted_iota(jnp.int32, (2 * TOK, TOK), 0)
    select = jnp.where(slots == target, 1.0, 0.0).astype(BF16)

    sent += merge(1)
    sent += pass_on(0)
    gathered(0)
    background.pop("w")()
    rs_copies = project(0)
    sent += pass_on(1)
    gathered(1)
    rs_copies += project(1)
    for copy in rs_copies:
        copy.wait_recv()
    sent += rs_copies
    added = []
    for part in range(2):
        rows = state[part * 64 : (part + 1) * 64, :]
        for i in range(3):
            rows += rrecv[part, i].astype(F32)
        added.append(rows)
    total = jnp.concatenate(added, axis=0)

    def three_terms(number, lanes, start):
        high = number.astype(BF16).astype(F32)
        rest = number - high
        middle = rest.astype(BF16).astype(F32)
        low = rest - middle
        return jnp.where(
            lanes == start,
            high,
            jnp.where(
                lanes == start + 1, middle, jnp.where(lanes == start + 2, low, 0.0)
            ),
        ).astype(BF16)

    squares = jnp.sum(total * total, axis=1, keepdims=True)
    pairs[:, 0:WIDTH] = (total * gain_ref[...]).astype(BF16)
    pairs[:, WIDTH:512] = three_terms(squares, lane, 64)[:, 64:128]
    dsend[...] = mm(select, pairs[...]).astype(BF16)
    experts = [(dy, dz) for dz in (1, 3, 2, 0) for dy in (2, 1, 3, 0)][:-1]
    d_copies = {}
    for i, (dy, dz) in enumerate(experts):
        peer = 4 * ((y + dy) % 4) + (zh + dz) % 4
        d_copies[dy, dz] = remote(
            dsend.at[aligned(peer * CAP, CAP)],
            drecv.at[0, 1 - dz % 2, aligned(e // 2 * CAP, CAP)],
            sem_d,
            i,
            (c, peer),
        )
        d_copies[dy, dz].start()
    drecv[0, 1, aligned(e // 2 * CAP, CAP), :] = dsend[aligned(e * CAP, CAP), :]
    d_forwards = []
    for part in range(2):
        for (dy, dz), copy in d_copies.items():
            if 1 - dz % 2 == part:
                copy.wait_recv()
        d_forwards.append(
            remote(drecv.at[0, part], drecv.at[1, part], sem_df, part, sibling)
        )
        d_forwards[-1].start()
    sent += list(d_copies.values()) + d_forwards

    background.pop("gu")()
    chip = 2 * x + zl
    own16 = aligned(chip * 16, 16)
    order = [(2, 1), (2, 0), (1, 1), (3, 1), (1, 0), (3, 0), (0, 1)]
    widths = (slice(0, HALF + 128), slice(0, HALF))
    p_copies = []
    for part in range(2):
        d_forwards[part].wait_recv()
        rows0 = drecv[0, part, :, 0:WIDTH]
        rows1 = drecv[1, part, :, 0:WIDTH]
        tail = drecv[0, part, :, 384:512].astype(F32) + drecv[
            1, part, :, 384:512
        ].astype(F32)
        squares = jnp.sum(jnp.where(lane >= 64, tail, 0.0), axis=1, keepdims=True)
        psend[part, 0, :, HALF : HALF + 128] = three_terms(squares, lane, 0)
        for col in range(2):
            for side in range(2):
                lanes = slice(side * HALF + col * 512, side * HALF + (col + 1) * 512)
                psend[part, col, :, side * 512 : (side + 1) * 512] = (
                    mm(rows0, gubuf[0, :, lanes]) + mm(rows1, gubuf[1, :, lanes])
                ).astype(BF16)
            for i, (dx, dz) in enumerate(order):
                px, pz = (x + dx) % 4, (zl + dz) % 2
                rows = aligned((2 * px + pz) * 16, 16)
                copy = remote(
                    psend.at[part, col, rows, widths[col]],
                    precv.at[part, col, i, :, widths[col]],
                    sem_p,
                    (part * 2 + col) * 7 + i,
                    at(px, pz, k, y, zh),
                )
                copy.start()
                p_copies.append(copy)
    sent += p_copies

    def hid_rows(side, part, dx, dz):
        source = 2 * ((x + 4 - dx) % 4) + (zl + dz) % 2
        return hid.at[side, part, aligned(source * 16, 16)]

    h_copies = []
    hf_copies = []
    for part in range(2):
        for col in range(2):
            summed = psend[part, col, own16, widths[col]].astype(F32)
            for i in (6, 4, 5, 2, 3, 1, 0):
                p_copies[(part * 2 + col) * 7 + i].wait_recv()
                summed += precv[part, col, i, :, widths[col]].astype(F32)
            if col == 0:
                mean = jnp.sum(summed[:, HALF:], axis=1, keepdims=True) / D
                factor = lax.rsqrt(mean + 1e-6)
            gate = summed[:, 0:512] * factor
            up = summed[:, 512:HALF] * factor
            lanes = slice(col * 512, (col + 1) * 512)
            hid[0, part, own16, lanes] = (
                gate / (1.0 + jnp.exp(-gate)) * up
            ).astype(BF16)
            here = hid.at[0, part, own16, lanes]
            for i, (dx, dz) in enumerate(chips):
                device = at((x + dx) % 4, (zl + dz) % 2, k, y, zh)
                i += (part * 2 + col) * 7
                h_copies.append(remote(here, here, sem_h, i, device))
                h_copies[-1].start()
        hf_copies.append(
            remote(
                hid.at[0, part, own16],
                hid.at[1, part, own16],
                sem_hf,
                part * 8 + 7,
                sibling,
            )
        )
        hf_copies[-1].start()
    sent += h_copies
    background.pop("wd")()
    y_copies = []
    for part in range(2):
        copies = [hf_copies[part]]
        for i, (dx, dz) in enumerate(chips):
            there = hid_rows(0, part, dx, dz)
            for col in range(2):
                piece = there.at[:, col * 512 : (col + 1) * 512]
                remote(
                    piece, piece, sem_h, (part * 2 + col) * 7 + i, sibling
                ).wait_recv()
            copies.append(
                remote(
                    there, hid_rows(1, part, dx, dz), sem_hf, part * 8 + i, sibling
                )
            )
            copies[-1].start()
        down = mm_t(hid[0, part], wdbuf[:, mine])
        for copy in copies:
            copy.wait_recv()
        sent += copies
        down += mm_t(hid[1, part], wdbuf[:, other])
        ysend[part] = down.astype(BF16)

        for i, (dy, dz) in enumerate(experts):
            if 1 - dz % 2 == part:
                peer = 4 * ((y + dy) % 4) + (zh + dz) % 4
                copy = remote(
                    ysend.at[part, aligned(peer // 2 * CAP, CAP)],
                    yrecv.at[aligned(e * CAP, CAP)],
                    sem_y,
                    i,
                    (c, peer),
                )
                copy.start()
                y_copies.append(copy)
    yrecv[aligned(e * CAP, CAP), :] = ysend[1, aligned(e // 2 * CAP, CAP), :]
    for copy in y_copies:
        copy.wait_recv()
    sent += y_copies
    routed = lax.dot_general(
        yrecv[...], select, (((0,), (0,)), ((), ())), preferred_element_type=F32
    )
    out_ref[...] = (total.T + routed * rw_ref[...]).astype(BF16)

    for part in range(2):
        for d in range(4):

            @pl.when(jnp.logical_not(on_self(d)))
            def _():
                for copy in o_copies(d, part):
                    copy.wait_send()
    for copy in sent:
        copy.wait_send()


def per_device(
    queries,
    latent_cache,
    group_latent,
    w_absorb_k,
    value_absorb_weight,
    w_out,
    residual,
    norm_gain,
    routes,
    route_weight,
    w_gate,
    w_up,
    w_down,
):
    vmem = pl.BlockSpec(memory_space=pltpu.VMEM)
    hbm = pl.BlockSpec(memory_space=pl.ANY)
    dma = pltpu.SemaphoreType.DMA
    return pl.pallas_call(
        kernel,
        out_shape=jax.ShapeDtypeStruct((WIDTH, TOK), BF16),
        in_specs=[vmem] * 5 + [hbm] + [vmem] * 4 + [hbm] * 3,
        out_specs=vmem,
        scratch_shapes=[
            pltpu.VMEM((4, 6, TOK, 128), BF16),
            pltpu.VMEM((2, KW, 2 * KEYS), BF16),
            pltpu.VMEM((4, 2, HEADS * 64, KW), BF16),
            pltpu.VMEM((4, HEADS * 64, RANK), F32),
            pltpu.VMEM((4, HEADS * 64, 1), F32),
            pltpu.VMEM((4, HEADS * 64, 1), F32),
            pltpu.VMEM((2, 4, 64, HEADS * VD), BF16),
            pltpu.VMEM((2, 4, 8, 128), F32),
            pltpu.VMEM((2, 4, 64, HEADS * VD), BF16),
            pltpu.VMEM((2, 4, 8, 128), F32),
            pltpu.VMEM((2, 4, 4 * 64, HEADS * VD), BF16),
            pltpu.VMEM((4, WIDTH, HEADS * VD), BF16),
            pltpu.VMEM((4 * 64, WIDTH), F32),
            pltpu.VMEM((2, 4 * 64, WIDTH), BF16),
            pltpu.VMEM((2, 3, 64, WIDTH), BF16),
            pltpu.VMEM((TOK, WIDTH), F32),
            pltpu.VMEM((TOK, 512), BF16),
            pltpu.VMEM((2 * TOK, 512), BF16),
            pltpu.VMEM((2, 2, TOK, 512), BF16),
            pltpu.VMEM((2, WIDTH, FF), BF16),
            pltpu.VMEM((WIDTH, FF), BF16),
            pltpu.VMEM((2, 2, TOK, HALF + 128), BF16),
            pltpu.VMEM((2, 2, 7, 16, HALF + 128), BF16),
            pltpu.VMEM((2, 2, TOK, HALF), BF16),
            pltpu.VMEM((2, TOK, WIDTH), BF16),
            pltpu.VMEM((2 * TOK, WIDTH), BF16),
            dma((2, 4)),
            dma((2, 5)),
            dma((2, 4)),
            dma((2, 4)),
            dma,
            dma((2, 8)),
            dma((2, 8)),
            dma((2, 14)),
            dma((2, 16)),
            dma((2, 6)),
            dma((2, 15)),
            dma((2, 2)),
            dma((2, 28)),
            dma((2, 28)),
            dma((2, 16)),
            dma((2, 15)),
        ],
        compiler_params=pltpu.CompilerParams(
            collective_id=0, has_side_effects=True, vmem_limit_bytes=56 * 2**20
        ),
        name="layer",
    )(
        queries.transpose(1, 2, 0),
        latent_cache.T,
        group_latent.T,
        w_absorb_k,
        value_absorb_weight,
        w_out.T,
        residual.T,
        norm_gain.reshape(1, WIDTH),
        routes.T,
        route_weight.T,
        w_gate,
        w_up,
        w_down.transpose(0, 2, 1),
    ).T


def solution(mesh):
    in_specs = (
        P("ctx", "exp", None),
        P("ctx", None),
        P("ctx", None),
        P("exp", None, None),
        P("exp", None, None),
        P("exp", "ctx"),
        P("exp", "ctx"),
        P("ctx"),
        P("exp", None),
        P("exp", None),
        P("exp", "ctx", None),
        P("exp", "ctx", None),
        P("exp", None, "ctx"),
    )
    out_specs = P("exp", "ctx")
    return jax.shard_map(
        per_device, mesh=mesh, in_specs=in_specs, out_specs=out_specs, check_vma=False
    )
```
